128 devices in a mesh: patch: 16 (over x_lo, y, core), tensor: 8 (over z, x_hi).
Axes of the slice: x: 4 (x_hi: 2, x_lo: 2; x = x_hi * 2 + x_lo), y: 4, z: 4, core: 2. Of those that a mesh axis runs over, the one named last changes fastest.
Arguments:
- latent_first: bfloat16 [4096, 5120], P('patch', 'tensor'), may hold values from -6 to 6
- latent_second: bfloat16 [4096, 5120], P('patch', 'tensor'), may hold values from -6 to 6
- stale_keys: bfloat16 [4096, 3072], P('patch', 'tensor'), may hold values from -12 to 12, as said below
- stale_values: bfloat16 [4096, 3072], P('patch', 'tensor'), may hold values from -6 to 6
- w_query: bfloat16 [5120, 3072], P(None, 'tensor'), may hold values from -0.078125 to 0.078125
- w_key: bfloat16 [5120, 3072], P(None, 'tensor'), may hold values from -0.078125 to 0.078125
- w_value: bfloat16 [5120, 3072], P(None, 'tensor'), may hold values from -0.078125 to 0.078125
- w_output: bfloat16 [3072, 5120], P('tensor'), may hold values from -0.109375 to 0.109375
Outputs:
- out_first: bfloat16 [4096, 5120], P('patch', 'tensor')
- out_second: bfloat16 [4096, 5120], P('patch', 'tensor')
The draws below stay inside these ranges and needn't reach their ends.
Inputs may be any that keep to these rules, and one draw needn't show every extreme that they name: `stale_keys`: cached keys of every head.
All inputs are finite; a program needn't handle non-finite values.
Results may differ from the reference program's by a relative error of at most 0.009.
Values may be sent and summed in bfloat16 or wider, within the bound.
A program may use at most 128 MiB of HBM per device.

```python
import jax
import jax.numpy as jnp
from jax import lax

D = 5120
HEADS = 24
HD = 128
TOK_DEV = 256
TOKENS = 4096
N_PATCH = 16


def draw_stale_keys(key, part):
    key = jax.random.fold_in(key, 11)
    base = jax.random.normal(jax.random.fold_in(key, 1), (TOKENS, HEADS * HD), jnp.float32)
    base = jnp.clip(base, -6.0, 6.0)
    return (2.0 * base).astype(jnp.bfloat16)


def shard_levels(stream_key, dims, shards, least, high):
    loudness = 1.0
    for position, blocks in shards:
        draws = jax.random.uniform(jax.random.fold_in(jax.random.fold_in(stream_key, 6), position), (blocks,), jnp.float32, least / len(shards), high / len(shards))
        loudness = loudness * jnp.repeat(jnp.exp(draws), dims[position] // blocks).reshape((-1,) + (1,) * (len(dims) - 1 - position))
    return loudness


def noise(key, shape, spread, bound, pieces=(), held_as=jnp.bfloat16):
    gain = shard_levels(key, shape, pieces, -0.22, 0.18) if pieces else 1.0
    entries = jax.random.normal(key, shape, jnp.float32) * spread * gain
    return jnp.minimum(jnp.maximum(entries, -bound), bound).astype(held_as)


def setup_inputs(seed: int = 0) -> dict:
    splits = jax.random.split(jax.random.key(seed), 9)
    return {
        "latent_first": noise(splits[0], (TOKENS, D), 1.0, 6.0, ((0, 16), (1, 8))),
        "latent_second": noise(splits[1], (TOKENS, D), 1.0, 6.0, ((0, 16), (1, 8))),
        "stale_keys": draw_stale_keys(jax.random.fold_in(splits[8], 71), 0),
        "stale_values": noise(splits[3], (TOKENS, HEADS * HD), 1.0, 6.0, ((0, 16), (1, 8))),
        "w_query": noise(splits[4], (D, HEADS * HD), D ** -0.5, 0.078125, ((1, 8),)),
        "w_key": noise(splits[5], (D, HEADS * HD), D ** -0.5, 0.078125, ((1, 8),)),
        "w_value": noise(splits[6], (D, HEADS * HD), D ** -0.5, 0.078125, ((1, 8),)),
        "w_output": noise(splits[7], (HEADS * HD, D), (HEADS * HD) ** -0.5, 0.109375, ((0, 8),)),
    }


def head_norm(mat):
    shaped = mat.reshape(mat.shape[0], HEADS, HD)
    scaled = shaped * lax.rsqrt(lax.optimization_barrier(jnp.mean(shaped * shaped, axis=-1, keepdims=True)) + 1e-06)
    return scaled.astype(jnp.bfloat16)

def one_step(latent, cache_keys, cache_values, w_query, w_key, w_value, w_output):
    wide = latent.astype(jnp.float32)
    normed = (wide * lax.rsqrt(lax.optimization_barrier(jnp.mean(wide * wide, axis=-1, keepdims=True)) + 1e-06)).astype(jnp.bfloat16)
    query = head_norm(jnp.dot(normed, w_query, preferred_element_type=jnp.float32))
    keyed = head_norm(jnp.dot(normed, w_key, preferred_element_type=jnp.float32))
    valued = jnp.dot(normed, w_value, preferred_element_type=jnp.float32).astype(jnp.bfloat16).reshape(TOKENS, HEADS, HD)
    cache_k = cache_keys.reshape(TOKENS, HEADS, HD)
    cache_v = cache_values.reshape(TOKENS, HEADS, HD)

    def per_patch(index):
        start = (index * TOK_DEV).astype(jnp.int32)
        zero = jnp.int32(0)
        own_q = lax.dynamic_slice(query, (start, zero, zero), (TOK_DEV, HEADS, HD))
        own_k = lax.dynamic_slice(keyed, (start, zero, zero), (TOK_DEV, HEADS, HD))
        own_v = lax.dynamic_slice(valued, (start, zero, zero), (TOK_DEV, HEADS, HD))
        keys_all = lax.dynamic_update_slice(cache_k, own_k, (start, zero, zero))
        vals_all = lax.dynamic_update_slice(cache_v, own_v, (start, zero, zero))
        scores = jnp.einsum('qhd,khd->hqk', own_q.astype(jnp.float32), keys_all.astype(jnp.float32)) / jnp.sqrt(jnp.float32(HD))
        peak = lax.optimization_barrier(jnp.max(scores, axis=-1, keepdims=True))
        expo = jnp.exp(scores - peak)
        total = lax.optimization_barrier(jnp.sum(expo, axis=-1))
        weights = expo.astype(jnp.bfloat16)
        acc = jnp.einsum('hqk,khd->qhd', weights.astype(jnp.float32), vals_all.astype(jnp.float32))
        return (acc / jnp.transpose(total)[:, :, None]).astype(jnp.bfloat16).reshape(TOK_DEV, HEADS * HD)
    attended = lax.map(per_patch, jnp.arange(N_PATCH, dtype=jnp.int32)).reshape(TOKENS, HEADS * HD)
    out = wide + jnp.dot(attended, w_output, preferred_element_type=jnp.float32)
    return (out.astype(jnp.bfloat16), keyed.reshape(TOKENS, HEADS * HD), valued.reshape(TOKENS, HEADS * HD))

def reference(latent_first, latent_second, stale_keys, stale_values, w_query, w_key, w_value, w_output):
    out_first, keys_first, values_first = one_step(latent_first, stale_keys, stale_values, w_query, w_key, w_value, w_output)
    out_second, unused_k, unused_v = one_step(latent_second, keys_first, values_first, w_query, w_key, w_value, w_output)
    return (out_first, out_second)
```

```python
import functools
import math

import jax
import jax.numpy as jnp
from jax import lax
from jax.experimental import pallas as pl
from jax.experimental.pallas import tpu as pltpu
from jax.sharding import PartitionSpec as P

HD = 128
EPS = 1e-06
C = math.log2(math.e) / math.sqrt(HD)
BF = jnp.bfloat16
F32 = jnp.float32
Y_ORDER = (1, 3, 2)


def _dot(a, b):
    return jnp.dot(a, b, preferred_element_type=F32)


def _dot_nt(a, b):
    return lax.dot_general(a, b, (((1,), (1,)), ((), ())), preferred_element_type=F32)


def _kernel(
    lat1, lat2, sk, sv, wq, wk, wv, wo,
    out1, out2,
    X, W, ACC, SS, QG, KB, VB, OWN, PS, PR, ST, STR, AG, WOG, OACC, A2, L2,
    x_s, x_r, w_l, c_s, c_r, n_s, n_r, q_s, q_r, p_s, p_r, t_s, t_r, a_s, a_r,
    o1_s, o1_r, o2_s, o2_r, o3_s, o3_r, l_s,
):
    lats = (lat1, lat2)
    patch = lax.axis_index("patch")
    tens = lax.axis_index("tensor")
    xl, y, c = patch // 8, (patch // 2) % 4, patch % 2
    z, xh = tens // 2, tens % 2

    def y_peer(d):
        return (xl * 8 + ((y + d) % 4) * 2 + c, tens)

    def class_peer(j):
        nc = (c + j % 2) % 2
        nx = (xl + j // 2) % 2
        return (nx * 8 + y * 2 + nc, tens)

    def t_index(r):
        return ((z + r // 2) % 4) * 2 + (xh + r % 2) % 2

    def t_peer(r):
        return (patch, t_index(r))

    def mirror(r):
        return ((4 - r // 2) % 4) * 2 + r % 2

    def remote(src, dst, ssem, rsem, dev):
        return pltpu.make_async_remote_copy(
            src_ref=src, dst_ref=dst, send_sem=ssem, recv_sem=rsem,
            device_id=dev, device_id_type=pl.DeviceIdType.MESH,
        )

    T_ORDER = (1, 2, 6, 3, 7, 4, 5)
    sends = []

    bar = pltpu.get_barrier_semaphore()
    peers = [y_peer(d) for d in Y_ORDER] + [class_peer(j) for j in (1, 2, 3)] + [t_peer(r) for r in range(1, 8)]
    for dev in peers:
        pl.semaphore_signal(bar, inc=1, device_id=dev, device_id_type=pl.DeviceIdType.MESH)
    pl.semaphore_wait(bar, len(peers))

    def start_latents(s):
        for r in T_ORDER:
            cp = remote(lats[s], X.at[s, mirror(r)], x_s.at[s, r], x_r.at[s, mirror(r)], t_peer(r))
            cp.start()
            sends.append(cp)

    start_latents(0)
    own_lat = [pltpu.make_async_copy(lats[s], X.at[s, 0], x_r.at[s, 0]) for s in (0, 1)]
    for cp in own_lat:
        cp.start()

    own_k = pltpu.make_async_copy(sk, KB.at[0, pl.ds(1024, 256)], l_s.at[0])
    own_v = pltpu.make_async_copy(sv, VB.at[0, pl.ds(1024, 256)], l_s.at[1])
    own_k.start()
    own_v.start()
    for d in Y_ORDER:
        r = 4 - d
        for i, (src, buf) in enumerate(((sk, KB), (sv, VB))):
            cp = remote(src, buf.at[0, pl.ds(r * 256, 256)], c_s.at[i, d], c_r.at[i, r], y_peer(d))
            cp.start()
            sends.append(cp)

    for i in range(8):
        r = (0,) + T_ORDER
        r = r[i]
        rows = pl.ds(pl.multiple_of(t_index(r) * 640, 640), 640)
        for k, w in enumerate((wq, wk, wv)):
            pltpu.make_async_copy(w.at[rows], W.at[r, :, pl.ds(k * 384, 384)], w_l.at[r, k]).start()

    own_cols = pl.ds(pl.multiple_of(tens * 640, 640), 640)
    own_wo = pltpu.make_async_copy(wo.at[:, :, own_cols], WOG.at[:, 0], l_s.at[2])
    own_wo.start()

    def project(s):
        ACC[...] = jnp.zeros_like(ACC)
        SS[...] = jnp.zeros_like(SS)

        def chunk(i, carry):
            r = jnp.where(i < 3, i, jnp.where(i == 3, 6, jnp.where(i == 4, 3, jnp.where(i == 5, 7, i - 2))))
            remote(lats[s], X.at[s, r], x_s.at[s, 0], x_r.at[s, r], t_peer(1)).wait_recv()
            if s == 0:
                for k, w in enumerate((wq, wk, wv)):
                    pltpu.make_async_copy(
                        w.at[pl.ds(0, 640)], W.at[r, :, pl.ds(k * 384, 384)], w_l.at[r, k]
                    ).wait()
            x = X[s, r]
            xf = x.astype(F32)
            sq = xf * xf
            SS[...] += sq[:, :128] + sq[:, 128:256] + sq[:, 256:384] + sq[:, 384:512] + sq[:, 512:640]
            ACC[...] += _dot(x, W[r])
            return carry

        lax.fori_loop(0, 8, chunk, 0)

    def norms(s):
        inv = lax.rsqrt(jnp.sum(SS[...], axis=-1, keepdims=True) * (1.0 / 5120) + EPS)
        for h in range(3):
            cols = pl.ds(h * 128, 128)
            k = ACC[:, pl.ds(384 + h * 128, 128)] * inv
            k = (k * lax.rsqrt(jnp.mean(k * k, axis=-1, keepdims=True) + EPS)).astype(BF)
            KB[s, pl.ds(0, 256), cols] = k
            v = (ACC[:, pl.ds(768 + h * 128, 128)] * inv).astype(BF)
            VB[s, pl.ds(0, 256), cols] = v
            if s == 0:
                KB[1, pl.ds(1024, 256), cols] = k
                VB[1, pl.ds(1024, 256), cols] = v
        if s == 0:
            for d in Y_ORDER:
                r = 4 - d
                for i, buf in enumerate((KB, VB)):
                    cp = remote(
                        buf.at[1, pl.ds(1024, 256)], buf.at[1, pl.ds(r * 256, 256)],
                        n_s.at[i, d], n_r.at[i, r], y_peer(d),
                    )
                    cp.start()
                    sends.append(cp)
        for h in range(3):
            cols = pl.ds(h * 128, 128)
            q = ACC[:, cols] * inv
            QG[s, 0, :, cols] = (q * lax.rsqrt(jnp.mean(q * q, axis=-1, keepdims=True) + EPS)).astype(BF)
        for j in (3, 2, 1):
            cp = remote(QG.at[s, 0], QG.at[s, j], q_s.at[s, j], q_r.at[s, j], class_peer(j))
            cp.start()
            sends.append(cp)

    def wait_queries(s):
        for j in (1, 2, 3):
            remote(QG.at[s, 0], QG.at[s, j], q_s.at[s, j], q_r.at[s, j], class_peer(j)).wait_recv()

    lane = lax.broadcasted_iota(jnp.int32, (256, 128), 1)

    def send_partials(s, h):
        for j in (3, 2, 1):
            cp = remote(PS.at[s, h, j], PR.at[s, h, j], p_s.at[s, h, j], p_r.at[s, h, j], class_peer(j))
            cp.start()
            sends.append(cp)
            cp = remote(ST.at[s, h, j], STR.at[s, h, j], t_s.at[s, h, j], t_r.at[s, h, j], class_peer(j))
            cp.start()
            sends.append(cp)

    def attention_one():
        for h in range(3):
            cols = pl.ds(h * 128, 128)

            def per_class(j, carry):
                start = pl.multiple_of(jnp.where(j == 0, 0, 256), 256)
                q = QG[0, j, :, cols]
                sc = _dot_nt(q, KB[0, pl.ds(start, 1024), cols])
                m = jnp.max(sc, axis=-1, keepdims=True)
                p = jnp.exp2((sc - m) * C)
                l = jnp.sum(p, axis=-1, keepdims=True)
                a = _dot(p.astype(BF), VB[0, pl.ds(start, 1024), cols])
                PS[0, h, j] = a.astype(BF)
                both = jnp.where(lane == 0, l, m)
                ST[0, h, j] = both.T[:8]

                @pl.when(j == 0)
                def _():
                    OWN[h] = a

                return carry

            lax.fori_loop(0, 4, per_class, 0)
            send_partials(0, h)

    def attention_two(part):
        first = part == 0
        for h in range(3):
            cols = pl.ds(h * 128, 128)
            if first:
                blocks = ((0, 1, 0), (1, 3, 1024))
            else:
                blocks = ((0, 4, part * 256),)
            for j0, nj, row in blocks:
                q = QG[1, pl.ds(j0, nj), :, cols].reshape(nj * 256, 128)
                p = jnp.exp2(_dot_nt(q, KB[1, pl.ds(row, 256), cols]) * C)
                l = p[:, :128] + p[:, 128:]
                a = _dot(p.astype(BF), VB[1, pl.ds(row, 256), cols])
                rows = pl.ds(j0 * 256, nj * 256)
                if first:
                    A2[h, rows] = a
                    L2[h, rows] = l
                else:
                    A2[h, rows] += a
                    L2[h, rows] += l
            if part == Y_ORDER[-1]:
                OWN[h] = A2[h, pl.ds(0, 256)]
                for j in range(4):
                    rows = pl.ds(j * 256, 256)
                    PS[1, h, j] = A2[h, rows].astype(BF)
                    l = jnp.sum(L2[h, rows], axis=-1, keepdims=True)
                    ST[1, h, j] = jnp.broadcast_to(l, (256, 128)).T[:8]
                send_partials(1, h)

    def merge(s, h):
        for j in (1, 2, 3):
            remote(PS.at[s, h, j], PR.at[s, h, j], p_s.at[s, h, j], p_r.at[s, h, j], class_peer(j)).wait_recv()
            remote(ST.at[s, h, j], STR.at[s, h, j], t_s.at[s, h, j], t_r.at[s, h, j], class_peer(j)).wait_recv()
        stats = [ST[s, h, 0]] + [STR[s, h, j] for j in (1, 2, 3)]
        cols = [jnp.concatenate([st] * 16, axis=0).T for st in stats]
        accs = [OWN[h]] + [PR[s, h, j].astype(F32) for j in (1, 2, 3)]
        ls = [st[:, 0:1] for st in cols]
        if s == 0:
            ms = [st[:, 1:2] for st in cols]
            top = functools.reduce(jnp.maximum, ms)
            ws = [jnp.exp2((m - top) * C) for m in ms]
            total = sum(w * l for w, l in zip(ws, ls))
            acc = sum(w * a for w, a in zip(ws, accs))
        else:
            total = sum(ls)
            acc = sum(accs)
        AG[s, h, :, pl.ds(0, 128)] = (acc / total).astype(BF)
        for r in T_ORDER:
            m = mirror(r)
            cp = remote(
                AG.at[s, h, :, pl.ds(0, 128)], AG.at[s, h, :, pl.ds(m * 128, 128)],
                a_s.at[s, h, r], a_r.at[s, h, m], t_peer(r),
            )
            cp.start()
            sends.append(cp)

    def out_head(s, h):
        for r in T_ORDER:
            remote(
                AG.at[s, h, :, pl.ds(0, 128)], AG.at[s, h, :, pl.ds(r * 128, 128)],
                a_s.at[s, h, r], a_r.at[s, h, r], t_peer(r),
            ).wait_recv()
        part = _dot(AG[s, h], WOG[h].reshape(1024, 640))
        if h == 0:
            OACC[...] = part + X[s, 0].astype(F32)
        elif h == 1:
            OACC[...] += part
        else:
            (out1, out2)[s][...] = (OACC[...] + part).astype(BF)

    def wo_rows(yy):
        return pl.ds(pl.multiple_of((((y + yy) % 4) * 2 + c) * 16, 16), 16)

    def wo_first():
        for r in T_ORDER:
            m = mirror(r)
            cols = pl.ds(pl.multiple_of(t_index(r) * 640, 640), 640)
            cp = remote(wo.at[:, wo_rows(0), cols], WOG.at[:, m, wo_rows(0)], o1_s.at[r], o1_r.at[m], t_peer(r))
            cp.start()
            sends.append(cp)

    def wo_first_wait():
        for r in T_ORDER:
            remote(
                wo.at[:, wo_rows(0), pl.ds(0, 640)], WOG.at[:, r, wo_rows(0)], o1_s.at[r], o1_r.at[r], t_peer(r)
            ).wait_recv()

    def wo_piece(yy):
        return WOG.at[:, pl.ds(1, 7), wo_rows(yy)]

    def wo_third(yy):
        cp = remote(wo_piece(yy), wo_piece(yy), o3_s.at[yy], o3_r.at[yy], class_peer(1))
        cp.start()
        sends.append(cp)

    def wo_second():
        for d in Y_ORDER:
            cp = remote(wo_piece(0), wo_piece(0), o2_s.at[d], o2_r.at[4 - d], y_peer(d))
            cp.start()
            sends.append(cp)
        wo_third(0)

    def wo_relay():
        for r in Y_ORDER:
            remote(wo_piece(0), wo_piece(r), o2_s.at[r], o2_r.at[r], y_peer(r)).wait_recv()
            wo_third(r)

    def wo_last_wait():
        for yy in range(4):
            rows = pl.ds(pl.multiple_of((((y + yy) % 4) * 2 + (1 - c)) * 16, 16), 16)
            piece = WOG.at[:, pl.ds(1, 7), rows]
            remote(piece, piece, o3_s.at[yy], o3_r.at[yy], class_peer(1)).wait_recv()
        own_wo.wait()

    project(0)
    start_latents(1)
    wo_first()
    norms(0)
    own_k.wait()
    own_v.wait()
    for r in Y_ORDER:
        for i, (src, buf) in enumerate(((sk, KB), (sv, VB))):
            remote(src, buf.at[0, pl.ds(r * 256, 256)], c_s.at[i, r], c_r.at[i, r], y_peer(r)).wait_recv()
    wait_queries(0)
    attention_one()
    wo_first_wait()
    wo_second()
    for h in range(3):
        merge(0, h)
    project(1)
    norms(1)
    wait_queries(1)
    attention_two(0)
    wo_relay()
    for r in Y_ORDER:
        for i, buf in enumerate((KB, VB)):
            remote(
                buf.at[1, pl.ds(1024, 256)], buf.at[1, pl.ds(r * 256, 256)],
                n_s.at[i, r], n_r.at[i, r], y_peer(r),
            ).wait_recv()
        attention_two(r)
    wo_last_wait()
    for h in range(3):
        merge(1, h)
        out_head(0, h)
    for h in range(3):
        out_head(1, h)
    for cp in sends:
        cp.wait_send()


def _shards(latent_first, latent_second, stale_keys, stale_values, w_query, w_key, w_value, w_output):
    dma = pltpu.SemaphoreType.DMA
    vm = pltpu.VMEM
    scratch = [
        vm((2, 8, 256, 640), BF),
        vm((8, 640, 1152), BF),
        vm((256, 1152), F32),
        vm((256, 128), F32),
        vm((2, 4, 256, 384), BF),
        vm((2, 1280, 384), BF),
        vm((2, 1280, 384), BF),
        vm((3, 256, 128), F32),
        vm((2, 3, 4, 256, 128), BF),
        vm((2, 3, 4, 256, 128), BF),
        vm((2, 3, 4, 8, 256), F32),
        vm((2, 3, 4, 8, 256), F32),
        vm((2, 3, 256, 1024), BF),
        vm((3, 8, 128, 640), BF),
        vm((256, 640), F32),
        vm((3, 1024, 128), F32),
        vm((3, 1024, 128), F32),
        dma((2, 8)), dma((2, 8)),
        dma((8, 3)),
        dma((2, 4)), dma((2, 4)),
        dma((2, 4)), dma((2, 4)),
        dma((2, 4)), dma((2, 4)),
        dma((2, 3, 4)), dma((2, 3, 4)),
        dma((2, 3, 4)), dma((2, 3, 4)),
        dma((2, 3, 8)), dma((2, 3, 8)),
        dma((8,)), dma((8,)),
        dma((4,)), dma((4,)),
        dma((4,)), dma((4,)),
        dma((3,)),
    ]
    out = jax.ShapeDtypeStruct((256, 640), BF)
    return pl.pallas_call(
        _kernel,
        out_shape=(out, out),
        in_specs=[pl.BlockSpec(memory_space=pl.ANY)] * 8,
        out_specs=(pl.BlockSpec(memory_space=pltpu.VMEM),) * 2,
        scratch_shapes=scratch,
        compiler_params=pltpu.CompilerParams(
            collective_id=0, has_side_effects=True, vmem_limit_bytes=60 * 2**20
        ),
        cost_estimate=pl.CostEstimate(flops=11_300_000_000, bytes_accessed=20_000_000, transcendentals=6_300_000),
        name="patch_attention",
    )(
        latent_first, latent_second, stale_keys, stale_values,
        w_query, w_key, w_value, w_output.reshape(3, 128, 5120),
    )


def solution(mesh):
    in_specs = (
        P("patch", "tensor"),
        P("patch", "tensor"),
        P("patch", "tensor"),
        P("patch", "tensor"),
        P(None, "tensor"),
        P(None, "tensor"),
        P(None, "tensor"),
        P("tensor", None),
    )
    out_specs = (P("patch", "tensor"), P("patch", "tensor"))
    return jax.shard_map(_shards, mesh=mesh, in_specs=in_specs, out_specs=out_specs, check_vma=False)
```

```python
import functools
import math

import jax
import jax.numpy as jnp
from jax import lax
from jax.experimental import pallas as pl
from jax.experimental.pallas import tpu as pltpu
from jax.sharding import PartitionSpec as P

HD = 128
EPS = 1e-06
C = math.log2(math.e) / math.sqrt(HD)
BF = jnp.bfloat16
F32 = jnp.float32
Y_ORDER = (1, 3, 2)


def _dot(a, b):
    return jnp.dot(a, b, preferred_element_type=F32)


def _dot_nt(a, b):
    return lax.dot_general(a, b, (((1,), (1,)), ((), ())), preferred_element_type=F32)


def _kernel(
    lat1, lat2, sk, sv, wq, wk, wv, wo,
    out1, out2,
    X, W, ACC, SS, QG, KB, VB, OWN, PS, PR, ST, STR, AG, WOG, OACC, A2, L2,
    x_s, x_r, w_l, c_s, c_r, n_s, n_r, q_s, q_r, p_s, p_r, t_s, t_r, a_s, a_r,
    o1_s, o1_r, o2_s, o2_r, o3_s, o3_r, l_s,
):
    lats = (lat1, lat2)
    patch = lax.axis_index("patch")
    tens = lax.axis_index("tensor")
    xl, y, c = patch // 8, (patch // 2) % 4, patch % 2
    z, xh = tens // 2, tens % 2

    def y_peer(d):
        return (xl * 8 + ((y + d) % 4) * 2 + c, tens)

    def class_peer(j):
        nc = (c + j % 2) % 2
        nx = (xl + j // 2) % 2
        return (nx * 8 + y * 2 + nc, tens)

    def t_index(r):
        return ((z + r // 2) % 4) * 2 + (xh + r % 2) % 2

    def t_peer(r):
        return (patch, t_index(r))

    def mirror(r):
        return ((4 - r // 2) % 4) * 2 + r % 2

    def remote(src, dst, ssem, rsem, dev):
        return pltpu.make_async_remote_copy(
            src_ref=src, dst_ref=dst, send_sem=ssem, recv_sem=rsem,
            device_id=dev, device_id_type=pl.DeviceIdType.MESH,
        )

    T_ORDER = (1, 2, 6, 3, 7, 4, 5)
    SLOTS = (0, 1, 4, 2, 6, 5, 3, 7)
    sends = []
    pending = {}

    def send(key, src, dst, ssem, rsem, dev, here, here_sem):
        cp = remote(src, dst, ssem, rsem, dev)
        cp.start()
        sends.append(cp)
        pending[key] = remote(here, here, here_sem, here_sem, t_peer(1))

    def take(*key):
        pending.pop(key).wait_recv()

    bar = pltpu.get_barrier_semaphore()
    peers = [y_peer(d) for d in Y_ORDER] + [class_peer(j) for j in (1, 2, 3)] + [t_peer(r) for r in range(1, 8)]
    for dev in peers:
        pl.semaphore_signal(bar, inc=1, device_id=dev, device_id_type=pl.DeviceIdType.MESH)
    pl.semaphore_wait(bar, len(peers))

    def gather_send(key, own, at, ssem, rsem):
        for r in (1, 4, 2, 6):
            m = mirror(r)
            send(key + (r,), own, at(m), ssem(r), rsem(m), t_peer(r), at(r), rsem(r))

    def gather_pass_partner(key, at, ssem, rsem):
        take(*key, 1)
        for r, slot in ((2, 7), (6, 3)):
            send(key + (slot,), at(1), at(slot), ssem(slot), rsem(slot), t_peer(r), at(slot), rsem(slot))

    def gather_pass_opposite(key, at, ssem, rsem):
        take(*key, 4)
        send(key + (5,), at(4), at(5), ssem(5), rsem(5), t_peer(1), at(5), rsem(5))

    def latents_at(s):
        return ("x", s), (lambda r: X.at[s, r]), (lambda r: x_s.at[s, r]), (lambda r: x_r.at[s, r])

    def start_latents(s):
        key, at, ssem, rsem = latents_at(s)
        gather_send(key, lats[s], at, ssem, rsem)

    def attended_at(s, h):
        return (
            ("a", s, h), (lambda r: AG.at[s, h, :, pl.ds(r * 128, 128)]),
            (lambda r: a_s.at[s, h, r]), (lambda r: a_r.at[s, h, r]),
        )

    def start_attended(s, h):
        key, at, ssem, rsem = attended_at(s, h)
        gather_send(key, at(0), at, ssem, rsem)

    start_latents(0)
    own_lat = [pltpu.make_async_copy(lats[s], X.at[s, 0], x_r.at[s, 0]) for s in (0, 1)]
    for cp in own_lat:
        cp.start()

    own_k = pltpu.make_async_copy(sk, KB.at[0, pl.ds(1024, 256)], l_s.at[0])
    own_v = pltpu.make_async_copy(sv, VB.at[0, pl.ds(1024, 256)], l_s.at[1])
    own_k.start()
    own_v.start()
    for d in Y_ORDER:
        r = 4 - d
        for i, (src, buf) in enumerate(((sk, KB), (sv, VB))):
            here = pl.ds(r * 256, 256)
            send(("c", i, r), src, buf.at[0, here], c_s.at[i, d], c_r.at[i, r], y_peer(d), buf.at[0, here], c_r.at[i, r])

    w_copies = {}
    for r in SLOTS:
        w_copies[r] = []
        rows = pl.ds(pl.multiple_of(t_index(r) * 640, 640), 640)
        for k, w in enumerate((wq, wk, wv)):
            copy = pltpu.make_async_copy(w.at[rows], W.at[r, :, pl.ds(k * 384, 384)], w_l.at[r, k])
            copy.start()
            w_copies[r].append(copy)

    own_cols = pl.ds(pl.multiple_of(tens * 640, 640), 640)
    own_wo = pltpu.make_async_copy(wo.at[:, :, own_cols], WOG.at[:, 0], l_s.at[2])
    own_wo.start()

    def project(s):
        if s == 0:
            gather_pass_partner(*latents_at(0))
            gather_pass_opposite(*latents_at(0))
        for r in SLOTS:
            if r == 0:
                own_lat[s].wait()
            elif r not in (1, 4):
                if s == 0 and r == SLOTS[-1]:
                    start_latents(1)
                take("x", s, r)
            if s == 0:
                for copy in w_copies[r]:
                    copy.wait()
            x = X[s, r]
            xf = x.astype(F32)
            sq = xf * xf
            sq = sq[:, :128] + sq[:, 128:256] + sq[:, 256:384] + sq[:, 384:512] + sq[:, 512:640]
            part = _dot(x, W[r])
            if r:
                SS[...] += sq
                ACC[...] += part
            else:
                SS[...] = sq
                ACC[...] = part

    def norms(s):
        inv = lax.rsqrt(jnp.sum(SS[...], axis=-1, keepdims=True) * (1.0 / 5120) + EPS)
        for h in range(3):
            cols = pl.ds(h * 128, 128)
            k = ACC[:, pl.ds(384 + h * 128, 128)] * inv
            k = (k * lax.rsqrt(jnp.mean(k * k, axis=-1, keepdims=True) + EPS)).astype(BF)
            KB[s, pl.ds(0, 256), cols] = k
            v = (ACC[:, pl.ds(768 + h * 128, 128)] * inv).astype(BF)
            VB[s, pl.ds(0, 256), cols] = v
            if s == 0:
                KB[1, pl.ds(1024, 256), cols] = k
                VB[1, pl.ds(1024, 256), cols] = v
        if s == 0:
            for d in Y_ORDER:
                r = 4 - d
                for i, buf in enumerate((KB, VB)):
                    here = buf.at[1, pl.ds(r * 256, 256)]
                    send(
                        ("n", i, r), buf.at[1, pl.ds(1024, 256)], here,
                        n_s.at[i, d], n_r.at[i, r], y_peer(d), here, n_r.at[i, r],
                    )
        for h in range(3):
            cols = pl.ds(h * 128, 128)
            q = ACC[:, cols] * inv
            QG[s, 0, :, cols] = (q * lax.rsqrt(jnp.mean(q * q, axis=-1, keepdims=True) + EPS)).astype(BF)
        for j in (3, 2, 1):
            send(("q", s, j), QG.at[s, 0], QG.at[s, j], q_s.at[s, j], q_r.at[s, j], class_peer(j), QG.at[s, j], q_r.at[s, j])

    def wait_queries(s):
        for j in (1, 2, 3):
            take("q", s, j)

    lane = lax.broadcasted_iota(jnp.int32, (256, 128), 1)

    def send_partials(s, h):
        for j in (3, 2, 1):
            for name, src, dst, ssem, rsem in (("p", PS, PR, p_s, p_r), ("t", ST, STR, t_s, t_r)):
                at = (s, h, j)
                send((name,) + at, src.at[at], dst.at[at], ssem.at[at], rsem.at[at], class_peer(j), dst.at[at], rsem.at[at])

    def attention_one(h):
        if True:
            cols = pl.ds(h * 128, 128)

            def per_class(j, carry):
                start = pl.multiple_of(jnp.where(j == 0, 0, 256), 256)
                q = QG[0, j, :, cols]
                sc = _dot_nt(q, KB[0, pl.ds(start, 1024), cols])
                m = jnp.max(sc, axis=-1, keepdims=True)
                p = jnp.exp2((sc - m) * C)
                l = jnp.sum(p, axis=-1, keepdims=True)
                a = _dot(p.astype(BF), VB[0, pl.ds(start, 1024), cols])
                PS[0, h, j] = a.astype(BF)
                both = jnp.where(lane == 0, l, m)
                ST[0, h, j] = both.T[:8]

                @pl.when(j == 0)
                def _():
                    OWN[h] = a

                return carry

            lax.fori_loop(0, 4, per_class, 0)
            send_partials(0, h)

    def attention_two(part):
        first = part == 0
        for h in range(3):
            cols = pl.ds(h * 128, 128)
            if first:
                blocks = ((0, 1, 0), (1, 3, 1024))
            else:
                blocks = ((0, 4, part * 256),)
            for j0, nj, row in blocks:
                q = QG[1, pl.ds(j0, nj), :, cols].reshape(nj * 256, 128)
                p = jnp.exp2(_dot_nt(q, KB[1, pl.ds(row, 256), cols]) * C)
                l = p[:, :128] + p[:, 128:]
                a = _dot(p.astype(BF), VB[1, pl.ds(row, 256), cols])
                rows = pl.ds(j0 * 256, nj * 256)
                if first:
                    A2[h, rows] = a
                    L2[h, rows] = l
                else:
                    A2[h, rows] += a
                    L2[h, rows] += l
            if part == Y_ORDER[-1]:
                OWN[h] = A2[h, pl.ds(0, 256)]
                for j in range(4):
                    rows = pl.ds(j * 256, 256)
                    PS[1, h, j] = A2[h, rows].astype(BF)
                    l = jnp.sum(L2[h, rows], axis=-1, keepdims=True)
                    ST[1, h, j] = jnp.broadcast_to(l, (256, 128)).T[:8]
                send_partials(1, h)

    def merge(s, h):
        for j in (1, 2, 3):
            take("p", s, h, j)
            take("t", s, h, j)
        stats = [ST[s, h, 0]] + [STR[s, h, j] for j in (1, 2, 3)]
        cols = [jnp.concatenate([st] * 16, axis=0).T for st in stats]
        accs = [OWN[h]] + [PR[s, h, j].astype(F32) for j in (1, 2, 3)]
        ls = [st[:, 0:1] for st in cols]
        if s == 0:
            ms = [st[:, 1:2] for st in cols]
            top = functools.reduce(jnp.maximum, ms)
            ws = [jnp.exp2((m - top) * C) for m in ms]
            total = sum(w * l for w, l in zip(ws, ls))
            acc = sum(w * a for w, a in zip(ws, accs))
        else:
            total = sum(ls)
            acc = sum(accs)
        AG[s, h, :, pl.ds(0, 128)] = (acc / total).astype(BF)

    def out_head(s, h):
        for r in (2, 6, 5, 3, 7):
            take("a", s, h, r)
        part = _dot(AG[s, h], WOG[h].reshape(1024, 640))
        if h == 0:
            OACC[...] = part + X[s, 0].astype(F32)
        elif h == 1:
            OACC[...] += part
        else:
            (out1, out2)[s][...] = (OACC[...] + part).astype(BF)

    def wo_rows(yy):
        return pl.ds(pl.multiple_of((((y + yy) % 4) * 2 + c) * 16, 16), 16)

    def wo_first():
        for r in T_ORDER:
            m = mirror(r)
            cols = pl.ds(pl.multiple_of(t_index(r) * 640, 640), 640)
            send(
                ("o1", r), wo.at[:, wo_rows(0), cols], WOG.at[:, m, wo_rows(0)], o1_s.at[r], o1_r.at[m], t_peer(r),
                WOG.at[:, r, wo_rows(0)], o1_r.at[r],
            )

    def wo_first_wait():
        for r in T_ORDER:
            take("o1", r)

    def wo_piece(yy):
        return WOG.at[:, pl.ds(1, 7), wo_rows(yy)]

    def wo_third(yy):
        rows = pl.ds(pl.multiple_of((((y + yy) % 4) * 2 + (1 - c)) * 16, 16), 16)
        send(
            ("o3", yy), wo_piece(yy), wo_piece(yy), o3_s.at[yy], o3_r.at[yy], class_peer(1),
            WOG.at[:, pl.ds(1, 7), rows], o3_r.at[yy],
        )

    def wo_second():
        for d in Y_ORDER:
            r = 4 - d
            send(("o2", r), wo_piece(0), wo_piece(0), o2_s.at[d], o2_r.at[r], y_peer(d), wo_piece(r), o2_r.at[r])
        wo_third(0)

    def wo_relay():
        for r in Y_ORDER:
            take("o2", r)
            wo_third(r)

    def wo_last_wait():
        for yy in range(4):
            take("o3", yy)
        own_wo.wait()

    project(0)
    norms(0)
    own_k.wait()
    own_v.wait()
    for r in Y_ORDER:
        for i in range(2):
            take("c", i, r)
    wait_queries(0)
    attention_one(0)
    gather_pass_partner(*latents_at(1))
    attention_one(1)
    gather_pass_opposite(*latents_at(1))
    attention_one(2)
    for h in range(3):
        merge(0, h)
    project(1)
    norms(1)
    wo_first()
    for h in range(3):
        start_attended(0, h)
    wait_queries(1)
    attention_two(0)
    for h in range(3):
        gather_pass_partner(*attended_at(0, h))
        gather_pass_opposite(*attended_at(0, h))
    wo_first_wait()
    wo_second()
    for r in Y_ORDER:
        for i in range(2):
            take("n", i, r)
        attention_two(r)
    for h in range(3):
        merge(1, h)
        start_attended(1, h)
    wo_relay()
    for h in range(3):
        gather_pass_partner(*attended_at(1, h))
        gather_pass_opposite(*attended_at(1, h))
    wo_last_wait()
    for h in range(3):
        out_head(0, h)
    for h in range(3):
        out_head(1, h)
    for cp in sends:
        cp.wait_send()


def _shards(latent_first, latent_second, stale_keys, stale_values, w_query, w_key, w_value, w_output):
    dma = pltpu.SemaphoreType.DMA
    vm = pltpu.VMEM
    scratch = [
        vm((2, 8, 256, 640), BF),
        vm((8, 640, 1152), BF),
        vm((256, 1152), F32),
        vm((256, 128), F32),
        vm((2, 4, 256, 384), BF),
        vm((2, 1280, 384), BF),
        vm((2, 1280, 384), BF),
        vm((3, 256, 128), F32),
        vm((2, 3, 4, 256, 128), BF),
        vm((2, 3, 4, 256, 128), BF),
        vm((2, 3, 4, 8, 256), F32),
        vm((2, 3, 4, 8, 256), F32),
        vm((2, 3, 256, 1024), BF),
        vm((3, 8, 128, 640), BF),
        vm((256, 640), F32),
        vm((3, 1024, 128), F32),
        vm((3, 1024, 128), F32),
        dma((2, 8)), dma((2, 8)),
        dma((8, 3)),
        dma((2, 4)), dma((2, 4)),
        dma((2, 4)), dma((2, 4)),
        dma((2, 4)), dma((2, 4)),
        dma((2, 3, 4)), dma((2, 3, 4)),
        dma((2, 3, 4)), dma((2, 3, 4)),
        dma((2, 3, 8)), dma((2, 3, 8)),
        dma((8,)), dma((8,)),
        dma((4,)), dma((4,)),
        dma((4,)), dma((4,)),
        dma((3,)),
    ]
    out = jax.ShapeDtypeStruct((256, 640), BF)
    return pl.pallas_call(
        _kernel,
        out_shape=(out, out),
        in_specs=[pl.BlockSpec(memory_space=pl.ANY)] * 8,
        out_specs=(pl.BlockSpec(memory_space=pltpu.VMEM),) * 2,
        scratch_shapes=scratch,
        compiler_params=pltpu.CompilerParams(
            collective_id=0, has_side_effects=True, vmem_limit_bytes=60 * 2**20
        ),
        cost_estimate=pl.CostEstimate(flops=11_300_000_000, bytes_accessed=20_000_000, transcendentals=6_300_000),
        name="patch_attention",
    )(
        latent_first, latent_second, stale_keys, stale_values,
        w_query, w_key, w_value, w_output.reshape(3, 128, 5120),
    )


def solution(mesh):
    in_specs = (
        P("patch", "tensor"),
        P("patch", "tensor"),
        P("patch", "tensor"),
        P("patch", "tensor"),
        P(None, "tensor"),
        P(None, "tensor"),
        P(None, "tensor"),
        P("tensor", None),
    )
    out_specs = (P("patch", "tensor"), P("patch", "tensor"))
    return jax.shard_map(_shards, mesh=mesh, in_specs=in_specs, out_specs=out_specs, check_vma=False)
```

```python
import functools
import math

import jax
import jax.numpy as jnp
from jax import lax
from jax.experimental import pallas as pl
from jax.experimental.pallas import tpu as pltpu
from jax.sharding import PartitionSpec as P

HD = 128
EPS = 1e-06
C = math.log2(math.e) / math.sqrt(HD)
BF = jnp.bfloat16
F32 = jnp.float32
Y_ORDER = (1, 3, 2)


def _dot(a, b):
    return jnp.dot(a, b, preferred_element_type=F32)


def _dot_nt(a, b):
    return lax.dot_general(a, b, (((1,), (1,)), ((), ())), preferred_element_type=F32)


def _kernel(
    lat1, lat2, sk, sv, wq, wk, wv, wo,
    out1, out2,
    X, W, ACC, SS, QG, KB, VB, LA, LM, CS, CR, CST, CRT, PS, PR, PST, PRT, AG, WOG, OACC,
    x_s, x_r, w_l, c_s, c_r, n_s, n_r, q_s, q_r, p_s, p_r, t_s, t_r, g_s, g_r, u_s, u_r, a_s, a_r,
    o1_s, o1_r, o2_s, o2_r, o3_s, o3_r, l_s,
):
    lats = (lat1, lat2)
    patch = lax.axis_index("patch")
    tens = lax.axis_index("tensor")
    xl, y, c = patch // 8, (patch // 2) % 4, patch % 2
    z, xh = tens // 2, tens % 2

    def y_peer(d):
        return (xl * 8 + ((y + d) % 4) * 2 + c, tens)

    def class_peer(j):
        nc = (c + j % 2) % 2
        nx = (xl + j // 2) % 2
        return (nx * 8 + y * 2 + nc, tens)

    def t_index(r):
        return ((z + r // 2) % 4) * 2 + (xh + r % 2) % 2

    def t_peer(r):
        return (patch, t_index(r))

    def mirror(r):
        return ((4 - r // 2) % 4) * 2 + r % 2

    def remote(src, dst, ssem, rsem, dev):
        return pltpu.make_async_remote_copy(
            src_ref=src, dst_ref=dst, send_sem=ssem, recv_sem=rsem,
            device_id=dev, device_id_type=pl.DeviceIdType.MESH,
        )

    T_ORDER = (1, 2, 6, 3, 7, 4, 5)
    SLOTS = (0, 1, 4, 2, 6, 5, 3, 7)
    sends = []
    pending = {}

    def send(key, src, dst, ssem, rsem, dev, here, here_sem):
        cp = remote(src, dst, ssem, rsem, dev)
        cp.start()
        sends.append(cp)
        pending[key] = remote(here, here, here_sem, here_sem, t_peer(1))

    def take(*key):
        pending.pop(key).wait_recv()

    bar = pltpu.get_barrier_semaphore()
    peers = [y_peer(d) for d in Y_ORDER] + [class_peer(j) for j in (1, 2)] + [t_peer(r) for r in range(1, 8)]
    for dev in peers:
        pl.semaphore_signal(bar, inc=1, device_id=dev, device_id_type=pl.DeviceIdType.MESH)
    pl.semaphore_wait(bar, len(peers))

    def gather_send(key, own, at, ssem, rsem):
        for r in (2, 6, 1):
            m = mirror(r)
            send(key + (r,), own, at(m), ssem(r), rsem(m), t_peer(r), at(r), rsem(r))

    def gather_pass_sides(key, at, ssem, rsem):
        for r, half, to in ((2, 0, 6), (6, 1, 2)):
            n = 4 + 4 * half
            take(*key, r)
            send(key + (n,), at(r, half), at(4, half), ssem(n), rsem(n), t_peer(to), at(4, half), rsem(n))

    def gather_pass_partner(key, at, ssem, rsem):
        take(*key, 1)
        for r, slot in ((2, 7), (6, 3)):
            send(key + (slot,), at(1), at(slot), ssem(slot), rsem(slot), t_peer(r), at(slot), rsem(slot))

    def gather_pass_opposite(key, at, ssem, rsem):
        for half in (0, 1):
            n = 5 + 4 * half
            take(*key, n - 1)
            send(key + (n,), at(4, half), at(5, half), ssem(n), rsem(n), t_peer(1), at(5, half), rsem(n))

    def half_rows(half):
        return pl.ds(0, 256) if half is None else pl.ds(half * 128, 128)

    def latents_at(s):
        return (
            ("x", s), (lambda r, half=None: X.at[s, r, half_rows(half)]),
            (lambda n: x_s.at[s, n]), (lambda n: x_r.at[s, n]),
        )

    def start_latents(s):
        key, at, ssem, rsem = latents_at(s)
        gather_send(key, lats[s], at, ssem, rsem)

    def attended_at(s, h):
        return (
            ("a", s, h), (lambda r, half=None: AG.at[s, h, half_rows(half), pl.ds(r * 128, 128)]),
            (lambda n: a_s.at[s, h, n]), (lambda n: a_r.at[s, h, n]),
        )

    def start_attended(s, h):
        key, at, ssem, rsem = attended_at(s, h)
        gather_send(key, at(0), at, ssem, rsem)

    start_latents(0)
    own_lat = [pltpu.make_async_copy(lats[s], X.at[s, 0], x_r.at[s, 0]) for s in (0, 1)]
    for cp in own_lat:
        cp.start()

    own_k = pltpu.make_async_copy(sk, KB.at[0, pl.ds(1024, 256)], l_s.at[0])
    own_v = pltpu.make_async_copy(sv, VB.at[0, pl.ds(1024, 256)], l_s.at[1])
    own_k.start()
    own_v.start()
    for d in Y_ORDER:
        r = 4 - d
        for i, (src, buf) in enumerate(((sk, KB), (sv, VB))):
            here = pl.ds(r * 256, 256)
            send(("c", i, r), src, buf.at[0, here], c_s.at[i, d], c_r.at[i, r], y_peer(d), buf.at[0, here], c_r.at[i, r])

    w_copies = {}
    for r in SLOTS:
        w_copies[r] = []
        rows = pl.ds(pl.multiple_of(t_index(r) * 640, 640), 640)
        for k, w in enumerate((wq, wk, wv)):
            copy = pltpu.make_async_copy(w.at[rows], W.at[r, :, pl.ds(k * 384, 384)], w_l.at[r, k])
            copy.start()
            w_copies[r].append(copy)

    own_cols = pl.ds(pl.multiple_of(tens * 640, 640), 640)
    own_wo = pltpu.make_async_copy(wo.at[:, :, own_cols], WOG.at[:, 0], l_s.at[2])
    own_wo.start()

    def project(s, slots):
        for r in slots:
            if r == 0:
                own_lat[s].wait()
            elif r == 5:
                take("x", s, 5)
                take("x", s, 9)
            elif r in (3, 7):
                take("x", s, r)
            if s == 0:
                for copy in w_copies[r]:
                    copy.wait()
            x = X[s, r]
            xf = x.astype(F32)
            sq = xf * xf
            sq = sq[:, :128] + sq[:, 128:256] + sq[:, 256:384] + sq[:, 384:512] + sq[:, 512:640]
            part = _dot(x, W[r])
            if r:
                SS[...] += sq
                ACC[...] += part
            else:
                SS[...] = sq
                ACC[...] = part

    def norms(s):
        inv = lax.rsqrt(jnp.sum(SS[...], axis=-1, keepdims=True) * (1.0 / 5120) + EPS)
        for h in range(3):
            cols = pl.ds(h * 128, 128)
            k = ACC[:, pl.ds(384 + h * 128, 128)] * inv
            k = (k * lax.rsqrt(jnp.mean(k * k, axis=-1, keepdims=True) + EPS)).astype(BF)
            KB[s, pl.ds(0, 256), cols] = k
            v = (ACC[:, pl.ds(768 + h * 128, 128)] * inv).astype(BF)
            VB[s, pl.ds(0, 256), cols] = v
            if s == 0:
                KB[1, pl.ds(1024, 256), cols] = k
                VB[1, pl.ds(1024, 256), cols] = v
        if s == 0:
            for d in Y_ORDER:
                r = 4 - d
                for i, buf in enumerate((KB, VB)):
                    here = buf.at[1, pl.ds(r * 256, 256)]
                    send(
                        ("n", i, r), buf.at[1, pl.ds(1024, 256)], here,
                        n_s.at[i, d], n_r.at[i, r], y_peer(d), here, n_r.at[i, r],
                    )
        for h in range(3):
            cols = pl.ds(h * 128, 128)
            q = ACC[:, cols] * inv
            QG[s, 0, :, cols] = (q * lax.rsqrt(jnp.mean(q * q, axis=-1, keepdims=True) + EPS)).astype(BF)
        for j in (2, 1):
            send(("q", s, j), QG.at[s, 0], QG.at[s, j], q_s.at[s, j], q_r.at[s, j], class_peer(j), QG.at[s, j], q_r.at[s, j])

    def pass_queries(s):
        take("q", s, 2)
        send(("q", s, 3), QG.at[s, 2], QG.at[s, 3], q_s.at[s, 3], q_r.at[s, 3], class_peer(1), QG.at[s, 3], q_r.at[s, 3])

    lane = lax.broadcasted_iota(jnp.int32, (256, 128), 1)

    def pack(l, m):
        return jnp.where(lane == 0, l, m)

    def unpack(st):
        both = jnp.concatenate([st] * 16, axis=0).T
        return both[:, 0:1], both[:, 1:2]

    def attend(s, h, j):
        cols = pl.ds(h * 128, 128)
        rows = pl.ds(0 if j == 0 else 256, 1024)
        sc = _dot_nt(QG[s, j, :, cols], KB[s, rows, cols])
        if s == 0:
            m = jnp.max(sc, axis=-1, keepdims=True)
            p = jnp.exp2((sc - m) * C)
        else:
            m = 0.0
            p = jnp.exp2(sc * C)
        l = jnp.sum(p, axis=-1, keepdims=True)
        a = _dot(p.astype(BF), VB[s, rows, cols])
        if j in (0, 2):
            LA[s, h, j // 2] = a
            LM[s, h, j // 2] = pack(l, m)
        else:
            at = (s, h, j // 2)
            CS[at] = a
            CST[at] = pack(l, m).T[:8]
            for name, src, dst, ssem, rsem in (("g", CS, CR, g_s, g_r), ("u", CST, CRT, u_s, u_r)):
                send((name,) + at, src.at[at], dst.at[at], ssem.at[at], rsem.at[at], class_peer(1), dst.at[at], rsem.at[at])

    def add_up(s, parts):
        accs, ls, ms = zip(*parts)
        if s == 1:
            return sum(accs), sum(ls), 0.0
        top = functools.reduce(jnp.maximum, ms)
        ws = [jnp.exp2((m - top) * C) for m in ms]
        return sum(w * a for w, a in zip(ws, accs)), sum(w * l for w, l in zip(ws, ls)), top

    def local(s, h, k):
        both = LM[s, h, k]
        return LA[s, h, k], both[:, 0:1], both[:, 1:2]

    def from_core(s, h, k):
        take("g", s, h, k)
        take("u", s, h, k)
        return (CR[s, h, k],) + unpack(CRT[s, h, k])

    def combine(s, h):
        a, l, m = add_up(s, [local(s, h, 1), from_core(s, h, 1)])
        at = (s, h)
        PS[at] = a.astype(BF)
        PST[at] = pack(l, m).T[:8]
        for name, src, dst, ssem, rsem in (("p", PS, PR, p_s, p_r), ("t", PST, PRT, t_s, t_r)):
            send((name,) + at, src.at[at], dst.at[at], ssem.at[at], rsem.at[at], class_peer(2), dst.at[at], rsem.at[at])

    def merge(s, h):
        near = [local(s, h, 0), from_core(s, h, 0)]
        take("p", s, h)
        take("t", s, h)
        a, l, _ = add_up(s, near + [(PR[s, h].astype(F32),) + unpack(PRT[s, h])])
        AG[s, h, :, pl.ds(0, 128)] = (a / l).astype(BF)
        start_attended(s, h)

    def out_head(s, h):
        for n in (5, 9, 3, 7):
            take("a", s, h, n)
        part = _dot(AG[s, h], WOG[h].reshape(1024, 640))
        if h == 0:
            OACC[...] = part + X[s, 0].astype(F32)
        elif h == 1:
            OACC[...] += part
        else:
            (out1, out2)[s][...] = (OACC[...] + part).astype(BF)

    def wo_rows(yy):
        return pl.ds(pl.multiple_of((((y + yy) % 4) * 2 + c) * 16, 16), 16)

    def wo_first():
        for r in T_ORDER:
            m = mirror(r)
            cols = pl.ds(pl.multiple_of(t_index(r) * 640, 640), 640)
            send(
                ("o1", r), wo.at[:, wo_rows(0), cols], WOG.at[:, m, wo_rows(0)], o1_s.at[r], o1_r.at[m], t_peer(r),
                WOG.at[:, r, wo_rows(0)], o1_r.at[r],
            )

    def wo_first_wait():
        for r in T_ORDER:
            take("o1", r)

    def wo_piece(yy):
        return WOG.at[:, pl.ds(1, 7), wo_rows(yy)]

    def wo_third(yy):
        rows = pl.ds(pl.multiple_of((((y + yy) % 4) * 2 + (1 - c)) * 16, 16), 16)
        send(
            ("o3", yy), wo_piece(yy), wo_piece(yy), o3_s.at[yy], o3_r.at[yy], class_peer(1),
            WOG.at[:, pl.ds(1, 7), rows], o3_r.at[yy],
        )

    def wo_second():
        for d in Y_ORDER:
            r = 4 - d
            send(("o2", r), wo_piece(0), wo_piece(0), o2_s.at[d], o2_r.at[r], y_peer(d), wo_piece(r), o2_r.at[r])
        wo_third(0)

    def wo_relay():
        for r in Y_ORDER:
            take("o2", r)
            wo_third(r)

    def wo_last_wait():
        for yy in range(4):
            take("o3", yy)
        own_wo.wait()

    gather_pass_sides(*latents_at(0))
    gather_pass_partner(*latents_at(0))
    project(0, (0, 1, 2, 6))
    gather_pass_opposite(*latents_at(0))
    project(0, (4, 3))
    start_latents(1)
    project(0, (7, 5))
    norms(0)
    own_k.wait()
    own_v.wait()
    for r in Y_ORDER:
        for i in range(2):
            take("c", i, r)
    for h in range(3):
        attend(0, h, 0)
    gather_pass_sides(*latents_at(1))
    gather_pass_partner(*latents_at(1))
    pass_queries(0)
    project(1, (0, 1, 2, 6))
    gather_pass_opposite(*latents_at(1))
    take("q", 0, 1)
    for h in range(3):
        attend(0, h, 1)
    take("q", 0, 3)
    for h in range(3):
        attend(0, h, 3)
        attend(0, h, 2)
    for h in range(3):
        combine(0, h)
    project(1, (4, 3))
    wo_first()
    project(1, (7, 5))
    norms(1)
    for r in Y_ORDER:
        for i in range(2):
            take("n", i, r)
    for h in range(3):
        attend(1, h, 0)
    take("q", 1, 1)
    for h in range(3):
        attend(1, h, 1)
    pass_queries(1)
    for h in range(3):
        merge(0, h)
    wo_first_wait()
    wo_second()
    take("q", 1, 3)
    for h in range(3):
        attend(1, h, 3)
        attend(1, h, 2)
    for h in range(3):
        combine(1, h)
    for h in range(3):
        gather_pass_sides(*attended_at(0, h))
        gather_pass_partner(*attended_at(0, h))
    for h in range(3):
        merge(1, h)
    for h in range(3):
        gather_pass_opposite(*attended_at(0, h))
    for h in range(3):
        gather_pass_sides(*attended_at(1, h))
        gather_pass_partner(*attended_at(1, h))
    wo_relay()
    for h in range(3):
        gather_pass_opposite(*attended_at(1, h))
    wo_last_wait()
    for h in range(3):
        out_head(0, h)
    for h in range(3):
        out_head(1, h)
    for cp in sends:
        cp.wait_send()


def _shards(latent_first, latent_second, stale_keys, stale_values, w_query, w_key, w_value, w_output):
    dma = pltpu.SemaphoreType.DMA
    vm = pltpu.VMEM
    scratch = [
        vm((2, 8, 256, 640), BF),
        vm((8, 640, 1152), BF),
        vm((256, 1152), F32),
        vm((256, 128), F32),
        vm((2, 4, 256, 384), BF),
        vm((2, 1280, 384), BF),
        vm((2, 1280, 384), BF),
        vm((2, 3, 2, 256, 128), F32),
        vm((2, 3, 2, 256, 128), F32),
        vm((2, 3, 2, 256, 128), F32),
        vm((2, 3, 2, 256, 128), F32),
        vm((2, 3, 2, 8, 256), F32),
        vm((2, 3, 2, 8, 256), F32),
        vm((2, 3, 256, 128), BF),
        vm((2, 3, 256, 128), BF),
        vm((2, 3, 8, 256), F32),
        vm((2, 3, 8, 256), F32),
        vm((2, 3, 256, 1024), BF),
        vm((3, 8, 128, 640), BF),
        vm((256, 640), F32),
        dma((2, 10)), dma((2, 10)),
        dma((8, 3)),
        dma((2, 4)), dma((2, 4)),
        dma((2, 4)), dma((2, 4)),
        dma((2, 4)), dma((2, 4)),
        dma((2, 3)), dma((2, 3)),
        dma((2, 3)), dma((2, 3)),
        dma((2, 3, 2)), dma((2, 3, 2)),
        dma((2, 3, 2)), dma((2, 3, 2)),
        dma((2, 3, 10)), dma((2, 3, 10)),
        dma((8,)), dma((8,)),
        dma((4,)), dma((4,)),
        dma((4,)), dma((4,)),
        dma((3,)),
    ]
    out = jax.ShapeDtypeStruct((256, 640), BF)
    return pl.pallas_call(
        _kernel,
        out_shape=(out, out),
        in_specs=[pl.BlockSpec(memory_space=pl.ANY)] * 8,
        out_specs=(pl.BlockSpec(memory_space=pltpu.VMEM),) * 2,
        scratch_shapes=scratch,
        compiler_params=pltpu.CompilerParams(
            collective_id=0, has_side_effects=True, vmem_limit_bytes=60 * 2**20
        ),
        cost_estimate=pl.CostEstimate(flops=11_300_000_000, bytes_accessed=20_000_000, transcendentals=6_300_000),
        name="patch_attention",
    )(
        latent_first, latent_second, stale_keys, stale_values,
        w_query, w_key, w_value, w_output.reshape(3, 128, 5120),
    )


def solution(mesh):
    in_specs = (
        P("patch", "tensor"),
        P("patch", "tensor"),
        P("patch", "tensor"),
        P("patch", "tensor"),
        P(None, "tensor"),
        P(None, "tensor"),
        P(None, "tensor"),
        P("tensor", None),
    )
    out_specs = (P("patch", "tensor"), P("patch", "tensor"))
    return jax.shard_map(_shards, mesh=mesh, in_specs=in_specs, out_specs=out_specs, check_vma=False)
```

```python
import functools
import math

import jax
import jax.numpy as jnp
from jax import lax
from jax.experimental import pallas as pl
from jax.experimental.pallas import tpu as pltpu
from jax.sharding import PartitionSpec as P

HD = 128
EPS = 1e-06
C = math.log2(math.e) / math.sqrt(HD)
BF = jnp.bfloat16
F32 = jnp.float32
Y_ORDER = (1, 3, 2)


def _dot(a, b):
    return jnp.dot(a, b, preferred_element_type=F32)


def _dot_nt(a, b):
    return lax.dot_general(a, b, (((1,), (1,)), ((), ())), preferred_element_type=F32)


def _kernel(
    lat1, lat2, sk, sv, wq, wk, wv, wo,
    out1, out2,
    X, W, ACC, SS, QG, KB, VB, LA, CS, CR, PS, PR, PST, PRT, AG, WOG, OACC,
    x_s, x_r, w_l, c_s, c_r, n_s, n_r, q_s, q_r, p_s, p_r, t_s, t_r, g_s, g_r, a_s, a_r,
    o1_s, o1_r, o2_s, o2_r, o3_s, o3_r, l_s,
):
    lats = (lat1, lat2)
    patch = lax.axis_index("patch")
    tens = lax.axis_index("tensor")
    xl, y, c = patch // 8, (patch // 2) % 4, patch % 2
    z, xh = tens // 2, tens % 2

    def y_peer(d):
        return (xl * 8 + ((y + d) % 4) * 2 + c, tens)

    def class_peer(j):
        nc = (c + j % 2) % 2
        nx = (xl + j // 2) % 2
        return (nx * 8 + y * 2 + nc, tens)

    def t_index(r):
        return ((z + r // 2) % 4) * 2 + (xh + r % 2) % 2

    def t_peer(r):
        return (patch, t_index(r))

    def mirror(r):
        return ((4 - r // 2) % 4) * 2 + r % 2

    def remote(src, dst, ssem, rsem, dev):
        return pltpu.make_async_remote_copy(
            src_ref=src, dst_ref=dst, send_sem=ssem, recv_sem=rsem,
            device_id=dev, device_id_type=pl.DeviceIdType.MESH,
        )

    T_ORDER = (1, 2, 6, 3, 7, 4, 5)
    SLOTS = (0, 1, 2, 6, 4, 3, 7, 5)
    PLACE = {r: i for i, r in enumerate(SLOTS)}

    def each_head(body):
        def step(h, carry):
            body(h)
            return carry

        lax.fori_loop(0, 3, step, 0)

    sends = []
    pending = {}

    def send(key, src, dst, ssem, rsem, dev, here, here_sem):
        cp = remote(src, dst, ssem, rsem, dev)
        cp.start()
        sends.append(cp)
        pending[key] = remote(here, here, here_sem, here_sem, t_peer(1))

    def take(*key):
        pending.pop(key).wait_recv()

    bar = pltpu.get_barrier_semaphore()
    peers = [y_peer(d) for d in Y_ORDER] + [class_peer(j) for j in (1, 2)] + [t_peer(r) for r in range(1, 8)]
    for dev in peers:
        pl.semaphore_signal(bar, inc=1, device_id=dev, device_id_type=pl.DeviceIdType.MESH)
    pl.semaphore_wait(bar, len(peers))

    OWN = ((0, None, 2, 6), (0, None, 6, 2), (0, None, 1, 1))
    SIDES = ((2, 0, 6, 4), (6, 1, 2, 4))
    PARTNER = ((1, None, 2, 7), (1, None, 6, 3))
    OPPOSITE = ((4, 0, 1, 5), (4, 1, 1, 5))

    def att_at(s, h, slot, half):
        return AG.at[s, h, half_rows(half), pl.ds(slot * 128, 128)]

    def att_copy(s, h, hop):
        slot, half, to, there = hop
        n = there + (4 if half else 0)
        return remote(att_at(s, h, slot, half), att_at(s, h, there, half), a_s.at[s, h, n], a_r.at[s, h, n], t_peer(to))

    def att_take(s, h, slot, half=None):
        n = slot + (4 if half else 0)
        here = att_at(s, h, slot, half)
        remote(here, here, a_s.at[s, h, n], a_r.at[s, h, n], t_peer(1)).wait_recv()

    def att_pass(s, h, hops, needs):
        for slot, half in needs:
            att_take(s, h, slot, half)
        for hop in hops:
            att_copy(s, h, hop).start()

    def att_first(s, h):
        att_pass(s, h, SIDES, ((2, None), (6, None)))
        att_pass(s, h, PARTNER, ((1, None),))

    def att_second(s, h):
        att_pass(s, h, OPPOSITE, ((4, 0), (4, 1)))

    def half_rows(half):
        return pl.ds(0, 256) if half is None else pl.ds(half * 128, 128)

    def lat_piece(s, slot, half):
        return X.at[s, PLACE[slot], half_rows(half)]

    def lat_send(s, src, to, slot, half):
        n = 2 * slot + half
        here = lat_piece(s, slot, half)
        send(("x", s, slot, half), src, here, x_s.at[s, n], x_r.at[s, n], t_peer(to), here, x_r.at[s, n])

    def start_latents(s):
        for r, half in ((2, 1), (6, 0), (1, 0), (2, 0), (6, 1), (1, 1)):
            lat_send(s, lats[s].at[half_rows(half)], r, mirror(r), half)

    def lat_sides(s):
        for slot, half, to in ((2, 0, 6), (6, 1, 2)):
            take("x", s, slot, half)
            lat_send(s, lat_piece(s, slot, half), to, 4, half)

    def lat_partner(s, half):
        take("x", s, 1, half)
        for to, slot in ((2, 7), (6, 3)):
            lat_send(s, lat_piece(s, 1, half), to, slot, half)

    def lat_opposite(s):
        for half in (0, 1):
            take("x", s, 4, half)
            lat_send(s, lat_piece(s, 4, half), 1, 5, half)

    def lat_opposite_z(s):
        for slot, half, to in ((3, 0, 6), (7, 1, 2)):
            take("x", s, slot, half)
            lat_send(s, lat_piece(s, slot, half), to, 5, half)

    start_latents(0)
    own_lat = [pltpu.make_async_copy(lats[s], X.at[s, 0], x_r.at[s, 0]) for s in (0, 1)]
    for cp in own_lat:
        cp.start()

    own_k = pltpu.make_async_copy(sk, KB.at[0, pl.ds(1024, 256)], l_s.at[0])
    own_v = pltpu.make_async_copy(sv, VB.at[0, pl.ds(1024, 256)], l_s.at[1])
    own_k.start()
    own_v.start()
    for d in Y_ORDER:
        r = 4 - d
        for i, (src, buf) in enumerate(((sk, KB), (sv, VB))):
            here = pl.ds(r * 256, 256)
            send(("c", i, r), src, buf.at[0, here], c_s.at[i, d], c_r.at[i, r], y_peer(d), buf.at[0, here], c_r.at[i, r])

    w_copies = {}
    for r in SLOTS:
        w_copies[r] = []
        rows = pl.ds(pl.multiple_of(t_index(r) * 640, 640), 640)
        for k, w in enumerate((wq, wk, wv)):
            copy = pltpu.make_async_copy(w.at[rows], W.at[PLACE[r], :, pl.ds(k * 384, 384)], w_l.at[r, k])
            copy.start()
            w_copies[r].append(copy)

    own_cols = pl.ds(pl.multiple_of(tens * 640, 640), 640)
    own_wo = pltpu.make_async_copy(wo.at[:, :, own_cols], WOG.at[:, 0], l_s.at[2])
    own_wo.start()

    def project(s, first, end):
        for r in SLOTS[first:end]:
            if r == 0:
                own_lat[s].wait()
            for half in (0, 1):
                if ("x", s, r, half) in pending:
                    take("x", s, r, half)
            if s == 0:
                for copy in w_copies[r]:
                    copy.wait()
        if first == 0:
            SS[...] = jnp.zeros_like(SS)
            ACC[...] = jnp.zeros_like(ACC)

        def chunk(i, carry):
            x = X[s, i]
            xf = x.astype(F32)
            sq = xf * xf
            SS[...] += sq[:, :128] + sq[:, 128:256] + sq[:, 256:384] + sq[:, 384:512] + sq[:, 512:640]
            ACC[...] += _dot(x, W[i])
            return carry

        lax.fori_loop(first, end, chunk, 0)

    def head_cols(h, base=0):
        return pl.ds(pl.multiple_of(base + h * 128, 128), 128)

    def norms(s):
        inv = lax.rsqrt(jnp.sum(SS[...], axis=-1, keepdims=True) * (1.0 / 5120) + EPS)

        def unit(x):
            x = x * inv
            return (x * lax.rsqrt(jnp.mean(x * x, axis=-1, keepdims=True) + EPS)).astype(BF)

        @each_head
        def _(h):
            cols = head_cols(h)
            k = unit(ACC[:, head_cols(h, 384)])
            v = (ACC[:, head_cols(h, 768)] * inv).astype(BF)
            KB[s, pl.ds(0, 256), cols] = k
            VB[s, pl.ds(0, 256), cols] = v
            if s == 0:
                KB[1, pl.ds(1024, 256), cols] = k
                VB[1, pl.ds(1024, 256), cols] = v

        if s == 0:
            for d in Y_ORDER:
                r = 4 - d
                for i, buf in enumerate((KB, VB)):
                    here = buf.at[1, pl.ds(r * 256, 256)]
                    send(
                        ("n", i, r), buf.at[1, pl.ds(1024, 256)], here,
                        n_s.at[i, d], n_r.at[i, r], y_peer(d), here, n_r.at[i, r],
                    )

        @each_head
        def _(h):
            QG[s, 0, :, head_cols(h)] = unit(ACC[:, head_cols(h)])

        for j in (2, 1):
            send(("q", s, j), QG.at[s, 0], QG.at[s, j], q_s.at[s, j], q_r.at[s, j], class_peer(j), QG.at[s, j], q_r.at[s, j])

    def pass_queries(s):
        take("q", s, 2)
        send(("q", s, 3), QG.at[s, 2], QG.at[s, 3], q_s.at[s, 3], q_r.at[s, 3], class_peer(1), QG.at[s, 3], q_r.at[s, 3])

    lane = lax.broadcasted_iota(jnp.int32, (256, 128), 1)

    def pack(l, m):
        return jnp.where(lane == 0, l, m)

    def unpack(st):
        both = jnp.concatenate([st] * 16, axis=0).T
        return both[:, 0:1], both[:, 1:2]

    def core_copy(s, h, k):
        at = (s, h, k)
        return remote(CS.at[at], CR.at[at], g_s.at[at], g_r.at[at], class_peer(1))

    def x_copies(s, h):
        at = (s, h)
        return (
            remote(PS.at[at], PR.at[at], p_s.at[at], p_r.at[at], class_peer(2)),
            remote(PST.at[at], PRT.at[at], t_s.at[at], t_r.at[at], class_peer(2)),
        )

    def attend(s, h, j):
        cols = head_cols(h)
        rows = [pl.ds(0 if i == 0 else 256, 1024) for i in (j, j + 1)]
        sc = [_dot_nt(QG[s, j + i, :, cols], KB[s, rows[i], cols]) for i in (0, 1)]
        m = [jnp.max(x, axis=-1, keepdims=True) if s == 0 else 0.0 for x in sc]
        p = [jnp.exp2((x - y) * C) if s == 0 else jnp.exp2(x * C) for x, y in zip(sc, m)]
        l = [jnp.sum(x, axis=-1, keepdims=True) for x in p]
        a = [_dot(p[i].astype(BF), VB[s, rows[i], cols]) for i in (0, 1)]
        k = j // 2
        CS[s, h, k, 0] = a[1]
        CS[s, h, k, 1] = pack(l[1], m[1])
        core_copy(s, h, k).start()
        LA[s, h, k, 0] = a[0]
        LA[s, h, k, 1] = pack(l[0], m[0])

    def add_up(s, parts):
        accs, ls, ms = zip(*parts)
        if s == 1:
            return sum(accs), sum(ls), 0.0
        top = functools.reduce(jnp.maximum, ms)
        ws = [jnp.exp2((m - top) * C) for m in ms]
        return sum(w * a for w, a in zip(ws, accs)), sum(w * l for w, l in zip(ws, ls)), top

    def near(s, h, k):
        core_copy(s, h, k).wait_recv()
        return [(ref[s, h, k, 0], ref[s, h, k, 1][:, 0:1], ref[s, h, k, 1][:, 1:2]) for ref in (LA, CR)]

    def combine(s, h):
        a, l, m = add_up(s, near(s, h, 1))
        PS[s, h] = a.astype(BF)
        PST[s, h] = pack(l, m).T[:8]
        for copy in x_copies(s, h):
            copy.start()

    def merge(s, h):
        parts = near(s, h, 0)
        for copy in x_copies(s, h):
            copy.wait_recv()
        a, l, _ = add_up(s, parts + [(PR[s, h].astype(F32),) + unpack(PRT[s, h])])
        AG[s, h, :, pl.ds(0, 128)] = (a / l).astype(BF)
        att_pass(s, h, OWN, ())

    def out_head(s, h):
        for slot, half in ((5, 0), (5, 1), (3, None), (7, None)):
            att_take(s, h, slot, half)
        OACC[...] += _dot(AG[s, h], WOG[h].reshape(1024, 640))

    def output(s):
        OACC[...] = jnp.zeros_like(OACC)
        each_head(functools.partial(out_head, s))
        (out1, out2)[s][...] = OACC[...]

    def settle(s):
        @each_head
        def _(h):
            for k in (0, 1):
                core_copy(s, h, k).wait_send()
            for copy in x_copies(s, h):
                copy.wait_send()
            for hop in OWN + SIDES + PARTNER + OPPOSITE:
                att_copy(s, h, hop).wait_send()

    def wo_rows(yy):
        return pl.ds(pl.multiple_of((((y + yy) % 4) * 2 + c) * 16, 16), 16)

    def wo_first():
        for r in T_ORDER:
            m = mirror(r)
            cols = pl.ds(pl.multiple_of(t_index(r) * 640, 640), 640)
            send(
                ("o1", r), wo.at[:, wo_rows(0), cols], WOG.at[:, m, wo_rows(0)], o1_s.at[r], o1_r.at[m], t_peer(r),
                WOG.at[:, r, wo_rows(0)], o1_r.at[r],
            )

    def wo_first_wait():
        for r in T_ORDER:
            take("o1", r)

    def wo_piece(yy):
        return WOG.at[:, pl.ds(1, 7), wo_rows(yy)]

    def wo_third(yy):
        rows = pl.ds(pl.multiple_of((((y + yy) % 4) * 2 + (1 - c)) * 16, 16), 16)
        send(
            ("o3", yy), wo_piece(yy), wo_piece(yy), o3_s.at[yy], o3_r.at[yy], class_peer(1),
            WOG.at[:, pl.ds(1, 7), rows], o3_r.at[yy],
        )

    def wo_second():
        for d in Y_ORDER:
            r = 4 - d
            send(("o2", r), wo_piece(0), wo_piece(0), o2_s.at[d], o2_r.at[r], y_peer(d), wo_piece(r), o2_r.at[r])
        wo_third(0)

    def wo_relay():
        for r in Y_ORDER:
            take("o2", r)
            wo_third(r)

    def wo_last_wait():
        for yy in range(4):
            take("o3", yy)
        own_wo.wait()

    def heads(fn, *args):
        each_head(lambda h: fn(args[0], h, *args[1:]))

    lat_sides(0)
    lat_partner(0, 0)
    lat_partner(0, 1)
    lat_opposite(0)
    wo_first()
    project(0, 0, 5)
    start_latents(1)
    project(0, 5, 8)
    norms(0)
    own_k.wait()
    own_v.wait()
    for r in Y_ORDER:
        for i in range(2):
            take("c", i, r)
    lat_sides(1)
    lat_partner(1, 0)
    take("q", 0, 1)
    heads(attend, 0, 0)
    lat_partner(1, 1)
    lat_opposite(1)
    pass_queries(0)
    project(1, 0, 4)
    take("q", 0, 3)
    heads(attend, 0, 2)
    wo_first_wait()
    wo_second()
    heads(combine, 0)
    project(1, 4, 8)
    norms(1)
    for r in Y_ORDER:
        for i in range(2):
            take("n", i, r)
    heads(merge, 0)
    take("q", 1, 1)
    heads(attend, 1, 0)
    pass_queries(1)
    heads(att_first, 0)
    take("q", 1, 3)
    heads(attend, 1, 2)
    heads(combine, 1)
    heads(merge, 1)
    heads(att_second, 0)
    heads(att_first, 1)
    wo_relay()
    heads(att_second, 1)
    settle(0)
    wo_last_wait()
    output(0)
    output(1)
    settle(1)
    for cp in sends:
        cp.wait_send()


def _shards(latent_first, latent_second, stale_keys, stale_values, w_query, w_key, w_value, w_output):
    dma = pltpu.SemaphoreType.DMA
    vm = pltpu.VMEM
    scratch = [
        vm((2, 8, 256, 640), BF),
        vm((8, 640, 1152), BF),
        vm((256, 1152), F32),
        vm((256, 128), F32),
        vm((2, 4, 256, 384), BF),
        vm((2, 1280, 384), BF),
        vm((2, 1280, 384), BF),
        vm((2, 3, 2, 2, 256, 128), F32),
        vm((2, 3, 2, 2, 256, 128), F32),
        vm((2, 3, 2, 2, 256, 128), F32),
        vm((2, 3, 256, 128), BF),
        vm((2, 3, 256, 128), BF),
        vm((2, 3, 8, 256), F32),
        vm((2, 3, 8, 256), F32),
        vm((2, 3, 256, 1024), BF),
        vm((3, 8, 128, 640), BF),
        vm((256, 640), F32),
        dma((2, 16)), dma((2, 16)),
        dma((8, 3)),
        dma((2, 4)), dma((2, 4)),
        dma((2, 4)), dma((2, 4)),
        dma((2, 4)), dma((2, 4)),
        dma((2, 3)), dma((2, 3)),
        dma((2, 3)), dma((2, 3)),
        dma((2, 3, 2)), dma((2, 3, 2)),
        dma((2, 3, 10)), dma((2, 3, 10)),
        dma((8,)), dma((8,)),
        dma((4,)), dma((4,)),
        dma((4,)), dma((4,)),
        dma((3,)),
    ]
    out = jax.ShapeDtypeStruct((256, 640), F32)
    sums = pl.pallas_call(
        _kernel,
        out_shape=(out, out),
        in_specs=[pl.BlockSpec(memory_space=pl.ANY)] * 8,
        out_specs=(pl.BlockSpec(memory_space=pltpu.VMEM),) * 2,
        scratch_shapes=scratch,
        compiler_params=pltpu.CompilerParams(
            collective_id=0, has_side_effects=True, vmem_limit_bytes=60 * 2**20
        ),
        cost_estimate=pl.CostEstimate(flops=11_300_000_000, bytes_accessed=20_000_000, transcendentals=6_300_000),
        name="patch_attention",
    )(
        latent_first, latent_second, stale_keys, stale_values,
        w_query, w_key, w_value, w_output.reshape(3, 128, 5120),
    )
    return tuple((x.astype(F32) + part).astype(BF) for x, part in zip((latent_first, latent_second), sums))


def solution(mesh):
    in_specs = (
        P("patch", "tensor"),
        P("patch", "tensor"),
        P("patch", "tensor"),
        P("patch", "tensor"),
        P(None, "tensor"),
        P(None, "tensor"),
        P(None, "tensor"),
        P("tensor", None),
    )
    out_specs = (P("patch", "tensor"), P("patch", "tensor"))
    return jax.shard_map(_shards, mesh=mesh, in_specs=in_specs, out_specs=out_specs, check_vma=False)
```

```python
import functools
import math

import jax
import jax.numpy as jnp
from jax import lax
from jax.experimental import pallas as pl
from jax.experimental.pallas import tpu as pltpu
from jax.sharding import PartitionSpec as P

HD = 128
EPS = 1e-06
C = math.log2(math.e) / math.sqrt(HD)
BF = jnp.bfloat16
F32 = jnp.float32
Y_ORDER = (1, 3, 2)


def _dot(a, b):
    return jnp.dot(a, b, preferred_element_type=F32)


def _dot_nt(a, b):
    return lax.dot_general(a, b, (((1,), (1,)), ((), ())), preferred_element_type=F32)


def _kernel(
    lat1, lat2, sk, sv, wq, wk, wv, wo,
    out1, out2,
    X, W, ACC, SS, QG, KB, VB, LA, CS, CR, PS, PR, PST, PRT, AG, WOG, OACC,
    x_s, x_r, w_l, c_s, c_r, n_s, n_r, q_s, q_r, p_s, p_r, t_s, t_r, g_s, g_r, a_s, a_r,
    o1_s, o1_r, o2_s, o2_r, o3_s, o3_r, l_s,
):
    lats = (lat1, lat2)
    patch = lax.axis_index("patch")
    tens = lax.axis_index("tensor")
    xl, y, c = patch // 8, (patch // 2) % 4, patch % 2
    z, xh = tens // 2, tens % 2

    def y_peer(d):
        return (xl * 8 + ((y + d) % 4) * 2 + c, tens)

    def class_peer(j):
        nc = (c + j % 2) % 2
        nx = (xl + j // 2) % 2
        return (nx * 8 + y * 2 + nc, tens)

    def t_index(r):
        return ((z + r // 2) % 4) * 2 + (xh + r % 2) % 2

    def t_peer(r):
        return (patch, t_index(r))

    def mirror(r):
        return ((4 - r // 2) % 4) * 2 + r % 2

    def remote(src, dst, ssem, rsem, dev):
        return pltpu.make_async_remote_copy(
            src_ref=src, dst_ref=dst, send_sem=ssem, recv_sem=rsem,
            device_id=dev, device_id_type=pl.DeviceIdType.MESH,
        )

    T_ORDER = (1, 2, 6, 3, 7, 4, 5)
    SLOTS = (0, 1, 2, 6, 4, 3, 7, 5)
    PLACE = {r: i for i, r in enumerate(SLOTS)}

    def each_head(body):
        def step(h, carry):
            body(h)
            return carry

        lax.fori_loop(0, 3, step, 0)

    sends = []
    pending = {}

    def send(key, src, dst, ssem, rsem, dev, here, here_sem):
        cp = remote(src, dst, ssem, rsem, dev)
        cp.start()
        sends.append(cp)
        pending[key] = remote(here, here, here_sem, here_sem, t_peer(1))

    def take(*key):
        pending.pop(key).wait_recv()

    bar = pltpu.get_barrier_semaphore()
    peers = [y_peer(d) for d in Y_ORDER] + [class_peer(j) for j in (1, 2)] + [t_peer(r) for r in range(1, 8)]
    for dev in peers:
        pl.semaphore_signal(bar, inc=1, device_id=dev, device_id_type=pl.DeviceIdType.MESH)
    pl.semaphore_wait(bar, len(peers))

    OWN = ((0, None, 2, 6), (0, None, 6, 2), (0, None, 1, 1))
    SIDES = ((2, 0, 6, 4), (6, 1, 2, 4))
    PARTNER = ((1, None, 2, 7), (1, None, 6, 3))
    OPPOSITE = ((4, 0, 1, 5), (4, 1, 1, 5))

    def att_at(s, h, slot, half):
        return AG.at[s, h, half_rows(half), pl.ds(slot * 128, 128)]

    def att_copy(s, h, hop):
        slot, half, to, there = hop
        n = there + (4 if half else 0)
        return remote(att_at(s, h, slot, half), att_at(s, h, there, half), a_s.at[s, h, n], a_r.at[s, h, n], t_peer(to))

    def att_take(s, h, slot, half=None):
        n = slot + (4 if half else 0)
        here = att_at(s, h, slot, half)
        remote(here, here, a_s.at[s, h, n], a_r.at[s, h, n], t_peer(1)).wait_recv()

    def att_pass(s, h, hops, needs):
        for slot, half in needs:
            att_take(s, h, slot, half)
        for hop in hops:
            att_copy(s, h, hop).start()

    def att_first(s, h):
        att_pass(s, h, SIDES, ((2, None), (6, None)))
        att_pass(s, h, PARTNER, ((1, None),))

    def att_second(s, h):
        att_pass(s, h, OPPOSITE, ((4, 0), (4, 1)))

    def half_rows(half):
        return pl.ds(0, 256) if half is None else pl.ds(half * 128, 128)

    def lat_piece(s, slot, half):
        return X.at[s, PLACE[slot], half_rows(half)]

    def lat_send(s, src, to, slot, half):
        n = 2 * slot + half
        here = lat_piece(s, slot, half)
        send(("x", s, slot, half), src, here, x_s.at[s, n], x_r.at[s, n], t_peer(to), here, x_r.at[s, n])

    def start_latents(s):
        for r, half in ((2, 1), (6, 0), (1, 0), (2, 0), (6, 1), (1, 1)):
            lat_send(s, lats[s].at[half_rows(half)], r, mirror(r), half)

    def lat_sides(s):
        for slot, half, to in ((2, 0, 6), (6, 1, 2)):
            take("x", s, slot, half)
            lat_send(s, lat_piece(s, slot, half), to, 4, half)

    def lat_partner(s, half):
        take("x", s, 1, half)
        for to, slot in ((2, 7), (6, 3)):
            lat_send(s, lat_piece(s, 1, half), to, slot, half)

    def lat_opposite(s):
        for half in (0, 1):
            take("x", s, 4, half)
            lat_send(s, lat_piece(s, 4, half), 1, 5, half)

    def lat_opposite_z(s):
        for slot, half, to in ((3, 0, 6), (7, 1, 2)):
            take("x", s, slot, half)
            lat_send(s, lat_piece(s, slot, half), to, 5, half)

    start_latents(0)
    own_lat = [pltpu.make_async_copy(lats[s], X.at[s, 0], x_r.at[s, 0]) for s in (0, 1)]
    for cp in own_lat:
        cp.start()

    own_k = pltpu.make_async_copy(sk, KB.at[0, pl.ds(1024, 256)], l_s.at[0])
    own_v = pltpu.make_async_copy(sv, VB.at[0, pl.ds(1024, 256)], l_s.at[1])
    own_k.start()
    own_v.start()
    for d in Y_ORDER:
        r = 4 - d
        for i, (src, buf) in enumerate(((sk, KB), (sv, VB))):
            here = pl.ds(r * 256, 256)
            send(("c", i, r), src, buf.at[0, here], c_s.at[i, d], c_r.at[i, r], y_peer(d), buf.at[0, here], c_r.at[i, r])

    w_copies = {}
    for r in SLOTS:
        w_copies[r] = []
        rows = pl.ds(pl.multiple_of(t_index(r) * 640, 640), 640)
        for k, w in enumerate((wq, wk, wv)):
            copy = pltpu.make_async_copy(w.at[rows], W.at[PLACE[r], :, pl.ds(k * 384, 384)], w_l.at[r, k])
            copy.start()
            w_copies[r].append(copy)

    own_cols = pl.ds(pl.multiple_of(tens * 640, 640), 640)
    own_wo = pltpu.make_async_copy(wo.at[:, :, own_cols], WOG.at[:, 0], l_s.at[2])
    own_wo.start()

    def project(s, first, end):
        for r in SLOTS[first:end]:
            if r == 0:
                own_lat[s].wait()
            for half in (0, 1):
                if ("x", s, r, half) in pending:
                    take("x", s, r, half)
            if s == 0:
                for copy in w_copies[r]:
                    copy.wait()
        if first == 0:
            SS[...] = jnp.zeros_like(SS)
            ACC[...] = jnp.zeros_like(ACC)

        def chunk(i, carry):
            x = X[s, i]
            xf = x.astype(F32)
            sq = xf * xf
            SS[...] += sq[:, :128] + sq[:, 128:256] + sq[:, 256:384] + sq[:, 384:512] + sq[:, 512:640]
            ACC[...] += _dot(x, W[i])
            return carry

        lax.fori_loop(first, end, chunk, 0)

    def head_cols(h, base=0):
        return pl.ds(pl.multiple_of(base + h * 128, 128), 128)

    def norms(s):
        inv = lax.rsqrt(jnp.sum(SS[...], axis=-1, keepdims=True) * (1.0 / 5120) + EPS)

        def unit(x):
            x = x * inv
            return (x * lax.rsqrt(jnp.mean(x * x, axis=-1, keepdims=True) + EPS)).astype(BF)

        def keys_values():
            @each_head
            def _(h):
                cols = head_cols(h)
                k = unit(ACC[:, head_cols(h, 384)])
                v = (ACC[:, head_cols(h, 768)] * inv).astype(BF)
                KB[s, pl.ds(0, 256), cols] = k
                VB[s, pl.ds(0, 256), cols] = v
                if s == 0:
                    KB[1, pl.ds(1024, 256), cols] = k
                    VB[1, pl.ds(1024, 256), cols] = v

        if s == 0:
            keys_values()
            for d in Y_ORDER:
                r = 4 - d
                for i, buf in enumerate((KB, VB)):
                    here = buf.at[1, pl.ds(r * 256, 256)]
                    send(
                        ("n", i, r), buf.at[1, pl.ds(1024, 256)], here,
                        n_s.at[i, d], n_r.at[i, r], y_peer(d), here, n_r.at[i, r],
                    )

        @each_head
        def _(h):
            QG[s, 0, :, head_cols(h)] = unit(ACC[:, head_cols(h)])
            for j in (2, 1):
                q_copy(s, h, j).start()

        if s == 1:
            keys_values()

    def q_copy(s, h, j):
        cols = head_cols(h)
        return remote(
            QG.at[s, 2 if j == 3 else 0, :, cols], QG.at[s, j, :, cols],
            q_s.at[s, j, h], q_r.at[s, j, h], class_peer(2 if j == 2 else 1),
        )

    def take_query(s, h, j):
        q_copy(s, h, j).wait_recv()

    def pass_query(s, h):
        take_query(s, h, 2)
        q_copy(s, h, 3).start()

    lane = lax.broadcasted_iota(jnp.int32, (256, 128), 1)

    def pack(l, m):
        return jnp.where(lane == 0, l, m)

    def unpack(st):
        both = jnp.concatenate([st] * 16, axis=0).T
        return both[:, 0:1], both[:, 1:2]

    def core_copy(s, h, k):
        at = (s, h, k)
        return remote(CS.at[at], CR.at[at], g_s.at[at], g_r.at[at], class_peer(1))

    def x_copies(s, h):
        at = (s, h)
        return (
            remote(PS.at[at], PR.at[at], p_s.at[at], p_r.at[at], class_peer(2)),
            remote(PST.at[at], PRT.at[at], t_s.at[at], t_r.at[at], class_peer(2)),
        )

    def attend(s, h, j):
        cols = head_cols(h)
        rows = [pl.ds(0 if i == 0 else 256, 1024) for i in (j, j + 1)]
        sc = [_dot_nt(QG[s, j + i, :, cols], KB[s, rows[i], cols]) for i in (0, 1)]
        m = [jnp.max(x, axis=-1, keepdims=True) if s == 0 else 0.0 for x in sc]
        p = [jnp.exp2((x - y) * C) if s == 0 else jnp.exp2(x * C) for x, y in zip(sc, m)]
        l = [jnp.sum(x, axis=-1, keepdims=True) for x in p]
        a = [_dot(p[i].astype(BF), VB[s, rows[i], cols]) for i in (0, 1)]
        k = j // 2
        CS[s, h, k, 0] = a[1]
        CS[s, h, k, 1] = pack(l[1], m[1])
        core_copy(s, h, k).start()
        LA[s, h, k, 0] = a[0]
        LA[s, h, k, 1] = pack(l[0], m[0])

    def add_up(s, parts):
        accs, ls, ms = zip(*parts)
        if s == 1:
            return sum(accs), sum(ls), 0.0
        top = functools.reduce(jnp.maximum, ms)
        ws = [jnp.exp2((m - top) * C) for m in ms]
        return sum(w * a for w, a in zip(ws, accs)), sum(w * l for w, l in zip(ws, ls)), top

    def near(s, h, k):
        core_copy(s, h, k).wait_recv()
        return [(ref[s, h, k, 0], ref[s, h, k, 1][:, 0:1], ref[s, h, k, 1][:, 1:2]) for ref in (LA, CR)]

    def combine(s, h):
        a, l, m = add_up(s, near(s, h, 1))
        PS[s, h] = a.astype(BF)
        PST[s, h] = pack(l, m).T[:8]
        for copy in x_copies(s, h):
            copy.start()

    def merge(s, h):
        parts = near(s, h, 0)
        for copy in x_copies(s, h):
            copy.wait_recv()
        a, l, _ = add_up(s, parts + [(PR[s, h].astype(F32),) + unpack(PRT[s, h])])
        AG[s, h, :, pl.ds(0, 128)] = (a / l).astype(BF)
        att_pass(s, h, OWN, ())

    def out_head(s, h):
        for slot, half in ((5, 0), (5, 1), (3, None), (7, None)):
            att_take(s, h, slot, half)
        OACC[...] += _dot(AG[s, h], WOG[h].reshape(1024, 640))

    def output(s):
        OACC[...] = jnp.zeros_like(OACC)
        each_head(functools.partial(out_head, s))
        (out1, out2)[s][...] = OACC[...]

    def settle(s):
        @each_head
        def _(h):
            for j in (1, 2, 3):
                q_copy(s, h, j).wait_send()
            for k in (0, 1):
                core_copy(s, h, k).wait_send()
            for copy in x_copies(s, h):
                copy.wait_send()
            for hop in OWN + SIDES + PARTNER + OPPOSITE:
                att_copy(s, h, hop).wait_send()

    def wo_rows(yy):
        return pl.ds(pl.multiple_of((((y + yy) % 4) * 2 + c) * 16, 16), 16)

    def wo_first():
        for r in T_ORDER:
            m = mirror(r)
            cols = pl.ds(pl.multiple_of(t_index(r) * 640, 640), 640)
            send(
                ("o1", r), wo.at[:, wo_rows(0), cols], WOG.at[:, m, wo_rows(0)], o1_s.at[r], o1_r.at[m], t_peer(r),
                WOG.at[:, r, wo_rows(0)], o1_r.at[r],
            )

    def wo_first_wait():
        for r in T_ORDER:
            take("o1", r)

    def wo_piece(yy):
        return WOG.at[:, pl.ds(1, 7), wo_rows(yy)]

    def wo_third(yy):
        rows = pl.ds(pl.multiple_of((((y + yy) % 4) * 2 + (1 - c)) * 16, 16), 16)
        send(
            ("o3", yy), wo_piece(yy), wo_piece(yy), o3_s.at[yy], o3_r.at[yy], class_peer(1),
            WOG.at[:, pl.ds(1, 7), rows], o3_r.at[yy],
        )

    def wo_second():
        for d in Y_ORDER:
            r = 4 - d
            send(("o2", r), wo_piece(0), wo_piece(0), o2_s.at[d], o2_r.at[r], y_peer(d), wo_piece(r), o2_r.at[r])
        wo_third(0)

    def wo_relay():
        for r in Y_ORDER:
            take("o2", r)
            wo_third(r)

    def wo_last_wait():
        for yy in range(4):
            take("o3", yy)
        own_wo.wait()

    def heads(fn, *args):
        each_head(lambda h: fn(args[0], h, *args[1:]))

    lat_sides(0)
    lat_partner(0, 0)
    lat_partner(0, 1)
    lat_opposite(0)
    wo_first()
    project(0, 0, 5)
    start_latents(1)
    project(0, 5, 8)
    norms(0)
    own_k.wait()
    own_v.wait()
    for r in Y_ORDER:
        for i in range(2):
            take("c", i, r)
    lat_sides(1)
    lat_partner(1, 0)
    heads(take_query, 0, 1)
    heads(attend, 0, 0)
    lat_partner(1, 1)
    lat_opposite(1)
    heads(pass_query, 0)
    project(1, 0, 4)
    heads(take_query, 0, 3)
    heads(attend, 0, 2)
    wo_first_wait()
    wo_second()
    heads(combine, 0)
    project(1, 4, 8)
    norms(1)
    for r in Y_ORDER:
        for i in range(2):
            take("n", i, r)
    heads(merge, 0)
    for h in range(3):
        take_query(1, h, 1)
        attend(1, h, 0)
        if h:
            pass_query(1, h - 1)
    pass_query(1, 2)
    for h in range(3):
        take_query(1, h, 3)
        attend(1, h, 2)
        if h:
            combine(1, h - 1)
    combine(1, 2)
    heads(att_first, 0)
    heads(merge, 1)
    heads(att_second, 0)
    heads(att_first, 1)
    wo_relay()
    heads(att_second, 1)
    settle(0)
    wo_last_wait()
    output(0)
    output(1)
    settle(1)
    for cp in sends:
        cp.wait_send()


def _shards(latent_first, latent_second, stale_keys, stale_values, w_query, w_key, w_value, w_output):
    dma = pltpu.SemaphoreType.DMA
    vm = pltpu.VMEM
    scratch = [
        vm((2, 8, 256, 640), BF),
        vm((8, 640, 1152), BF),
        vm((256, 1152), F32),
        vm((256, 128), F32),
        vm((2, 4, 256, 384), BF),
        vm((2, 1280, 384), BF),
        vm((2, 1280, 384), BF),
        vm((2, 3, 2, 2, 256, 128), F32),
        vm((2, 3, 2, 2, 256, 128), F32),
        vm((2, 3, 2, 2, 256, 128), F32),
        vm((2, 3, 256, 128), BF),
        vm((2, 3, 256, 128), BF),
        vm((2, 3, 8, 256), F32),
        vm((2, 3, 8, 256), F32),
        vm((2, 3, 256, 1024), BF),
        vm((3, 8, 128, 640), BF),
        vm((256, 640), F32),
        dma((2, 16)), dma((2, 16)),
        dma((8, 3)),
        dma((2, 4)), dma((2, 4)),
        dma((2, 4)), dma((2, 4)),
        dma((2, 4, 3)), dma((2, 4, 3)),
        dma((2, 3)), dma((2, 3)),
        dma((2, 3)), dma((2, 3)),
        dma((2, 3, 2)), dma((2, 3, 2)),
        dma((2, 3, 10)), dma((2, 3, 10)),
        dma((8,)), dma((8,)),
        dma((4,)), dma((4,)),
        dma((4,)), dma((4,)),
        dma((3,)),
    ]
    out = jax.ShapeDtypeStruct((256, 640), F32)
    sums = pl.pallas_call(
        _kernel,
        out_shape=(out, out),
        in_specs=[pl.BlockSpec(memory_space=pl.ANY)] * 8,
        out_specs=(pl.BlockSpec(memory_space=pltpu.VMEM),) * 2,
        scratch_shapes=scratch,
        compiler_params=pltpu.CompilerParams(
            collective_id=0, has_side_effects=True, vmem_limit_bytes=60 * 2**20
        ),
        cost_estimate=pl.CostEstimate(flops=11_300_000_000, bytes_accessed=20_000_000, transcendentals=6_300_000),
        name="patch_attention",
    )(
        latent_first, latent_second, stale_keys, stale_values,
        w_query, w_key, w_value, w_output.reshape(3, 128, 5120),
    )
    return tuple((x.astype(F32) + part).astype(BF) for x, part in zip((latent_first, latent_second), sums))


def solution(mesh):
    in_specs = (
        P("patch", "tensor"),
        P("patch", "tensor"),
        P("patch", "tensor"),
        P("patch", "tensor"),
        P(None, "tensor"),
        P(None, "tensor"),
        P(None, "tensor"),
        P("tensor", None),
    )
    out_specs = (P("patch", "tensor"), P("patch", "tensor"))
    return jax.shard_map(_shards, mesh=mesh, in_specs=in_specs, out_specs=out_specs, check_vma=False)
```

```python
import functools
import math

import jax
import jax.numpy as jnp
from jax import lax
from jax.experimental import pallas as pl
from jax.experimental.pallas import tpu as pltpu
from jax.sharding import PartitionSpec as P

HD = 128
EPS = 1e-06
C = math.log2(math.e) / math.sqrt(HD)
BF = jnp.bfloat16
F32 = jnp.float32
Y_ORDER = (1, 3, 2)


def _dot(a, b):
    return jnp.dot(a, b, preferred_element_type=F32)


def _dot_nt(a, b):
    return lax.dot_general(a, b, (((1,), (1,)), ((), ())), preferred_element_type=F32)


def _kernel(
    lat1, lat2, sk, sv, wq, wk, wv, wo,
    out1, out2,
    X, W, ACC, SS, QG, KB, VB, LA, CS, CR, PS, PR, PST, PRT, AG, WOG, OACC,
    x_s, x_r, w_l, c_s, c_r, n_s, n_r, q_s, q_r, p_s, p_r, t_s, t_r, g_s, g_r, a_s, a_r,
    o1_s, o1_r, o2_s, o2_r, o3_s, o3_r, l_s,
):
    lats = (lat1, lat2)
    patch = lax.axis_index("patch")
    tens = lax.axis_index("tensor")
    xl, y, c = patch // 8, (patch // 2) % 4, patch % 2
    z, xh = tens // 2, tens % 2

    def y_peer(d):
        return (xl * 8 + ((y + d) % 4) * 2 + c, tens)

    def class_peer(j):
        nc = (c + j % 2) % 2
        nx = (xl + j // 2) % 2
        return (nx * 8 + y * 2 + nc, tens)

    def t_index(r):
        return ((z + r // 2) % 4) * 2 + (xh + r % 2) % 2

    def t_peer(r):
        return (patch, t_index(r))

    def mirror(r):
        return ((4 - r // 2) % 4) * 2 + r % 2

    def remote(src, dst, ssem, rsem, dev):
        return pltpu.make_async_remote_copy(
            src_ref=src, dst_ref=dst, send_sem=ssem, recv_sem=rsem,
            device_id=dev, device_id_type=pl.DeviceIdType.MESH,
        )

    T_ORDER = (1, 2, 6, 3, 7, 4, 5)
    SLOTS = (0, 1, 2, 6, 4, 3, 7, 5)
    PLACE = {r: i for i, r in enumerate(SLOTS)}

    def each_head(body):
        def step(h, carry):
            body(h)
            return carry

        lax.fori_loop(0, 3, step, 0)

    sends = []
    pending = {}

    def send(key, src, dst, ssem, rsem, dev, here, here_sem):
        cp = remote(src, dst, ssem, rsem, dev)
        cp.start()
        sends.append(cp)
        pending[key] = remote(here, here, here_sem, here_sem, t_peer(1))

    def take(*key):
        pending.pop(key).wait_recv()

    bar = pltpu.get_barrier_semaphore()
    peers = [y_peer(d) for d in Y_ORDER] + [class_peer(j) for j in (1, 2)] + [t_peer(r) for r in range(1, 8)]
    for dev in peers:
        pl.semaphore_signal(bar, inc=1, device_id=dev, device_id_type=pl.DeviceIdType.MESH)
    pl.semaphore_wait(bar, len(peers))

    OWN = ((0, None, 2, 6), (0, None, 6, 2), (0, None, 1, 1))
    SIDES = ((2, 0, 6, 4), (6, 1, 2, 4))
    PARTNER = ((1, None, 2, 7), (1, None, 6, 3))
    OPPOSITE = ((4, 0, 1, 5), (4, 1, 1, 5))

    def att_at(s, h, slot, half):
        return AG.at[s, h, half_rows(half), pl.ds(slot * 128, 128)]

    def att_copy(s, h, hop):
        slot, half, to, there = hop
        n = there + (4 if half else 0)
        return remote(att_at(s, h, slot, half), att_at(s, h, there, half), a_s.at[s, h, n], a_r.at[s, h, n], t_peer(to))

    def att_take(s, h, slot, half=None):
        n = slot + (4 if half else 0)
        here = att_at(s, h, slot, half)
        remote(here, here, a_s.at[s, h, n], a_r.at[s, h, n], t_peer(1)).wait_recv()

    def att_pass(s, h, hops, needs):
        for slot, half in needs:
            att_take(s, h, slot, half)
        for hop in hops:
            att_copy(s, h, hop).start()

    def att_first(s, h):
        att_pass(s, h, SIDES, ((2, None), (6, None)))
        att_pass(s, h, PARTNER, ((1, None),))

    def att_second(s, h):
        att_pass(s, h, OPPOSITE, ((4, 0), (4, 1)))

    def half_rows(half):
        return pl.ds(0, 256) if half is None else pl.ds(half * 128, 128)

    def lat_piece(s, slot, half):
        return X.at[s, PLACE[slot], half_rows(half)]

    def lat_send(s, src, to, slot, half):
        n = 2 * slot + half
        here = lat_piece(s, slot, half)
        send(("x", s, slot, half), src, here, x_s.at[s, n], x_r.at[s, n], t_peer(to), here, x_r.at[s, n])

    def start_latents(s):
        for r, half in ((2, 1), (6, 0), (1, 0), (2, 0), (6, 1), (1, 1)):
            lat_send(s, lats[s].at[half_rows(half)], r, mirror(r), half)

    def lat_sides(s):
        for slot, half, to in ((2, 0, 6), (6, 1, 2)):
            take("x", s, slot, half)
            lat_send(s, lat_piece(s, slot, half), to, 4, half)

    def lat_partner(s, half):
        take("x", s, 1, half)
        for to, slot in ((2, 7), (6, 3)):
            lat_send(s, lat_piece(s, 1, half), to, slot, half)

    def lat_opposite(s):
        for half in (0, 1):
            take("x", s, 4, half)
            lat_send(s, lat_piece(s, 4, half), 1, 5, half)

    def lat_opposite_z(s):
        for slot, half, to in ((3, 0, 6), (7, 1, 2)):
            take("x", s, slot, half)
            lat_send(s, lat_piece(s, slot, half), to, 5, half)

    start_latents(0)
    own_lat = [pltpu.make_async_copy(lats[s], X.at[s, 0], x_r.at[s, 0]) for s in (0, 1)]
    for cp in own_lat:
        cp.start()

    own_k = pltpu.make_async_copy(sk, KB.at[0, pl.ds(1024, 256)], l_s.at[0])
    own_v = pltpu.make_async_copy(sv, VB.at[0, pl.ds(1024, 256)], l_s.at[1])
    own_k.start()
    own_v.start()
    for d in Y_ORDER:
        r = 4 - d
        for i, (src, buf) in enumerate(((sk, KB), (sv, VB))):
            here = pl.ds(r * 256, 256)
            send(("c", i, r), src, buf.at[0, here], c_s.at[i, d], c_r.at[i, r], y_peer(d), buf.at[0, here], c_r.at[i, r])

    w_copies = {}
    for r in SLOTS:
        w_copies[r] = []
        rows = pl.ds(pl.multiple_of(t_index(r) * 640, 640), 640)
        for k, w in enumerate((wq, wk, wv)):
            copy = pltpu.make_async_copy(w.at[rows], W.at[PLACE[r], :, pl.ds(k * 384, 384)], w_l.at[r, k])
            copy.start()
            w_copies[r].append(copy)

    own_cols = pl.ds(pl.multiple_of(tens * 640, 640), 640)
    own_wo = pltpu.make_async_copy(wo.at[:, :, own_cols], WOG.at[:, 0], l_s.at[2])
    own_wo.start()

    def project(s, first, end):
        for r in SLOTS[first:end]:
            if r == 0:
                own_lat[s].wait()
            for half in (0, 1):
                if ("x", s, r, half) in pending:
                    take("x", s, r, half)
            if s == 0:
                for copy in w_copies[r]:
                    copy.wait()
        if first == 0:
            SS[...] = jnp.zeros_like(SS)
            ACC[...] = jnp.zeros_like(ACC)

        def chunk(i, carry):
            x = X[s, i]
            xf = x.astype(F32)
            sq = xf * xf
            SS[...] += sq[:, :128] + sq[:, 128:256] + sq[:, 256:384] + sq[:, 384:512] + sq[:, 512:640]
            ACC[...] += _dot(x, W[i])
            return carry

        lax.fori_loop(first, end, chunk, 0)

    def head_cols(h, base=0):
        return pl.ds(pl.multiple_of(base + h * 128, 128), 128)

    def norms(s):
        inv = lax.rsqrt(jnp.sum(SS[...], axis=-1, keepdims=True) * (1.0 / 5120) + EPS)

        def unit(x):
            x = x * inv
            return (x * lax.rsqrt(jnp.mean(x * x, axis=-1, keepdims=True) + EPS)).astype(BF)

        def keys_values():
            @each_head
            def _(h):
                cols = head_cols(h)
                k = unit(ACC[:, head_cols(h, 384)])
                v = (ACC[:, head_cols(h, 768)] * inv).astype(BF)
                KB[s, pl.ds(0, 256), cols] = k
                VB[s, pl.ds(0, 256), cols] = v
                if s == 0:
                    KB[1, pl.ds(1024, 256), cols] = k
                    VB[1, pl.ds(1024, 256), cols] = v

        if s == 0:
            keys_values()
            for d in Y_ORDER:
                r = 4 - d
                for i, buf in enumerate((KB, VB)):
                    here = buf.at[1, pl.ds(r * 256, 256)]
                    send(
                        ("n", i, r), buf.at[1, pl.ds(1024, 256)], here,
                        n_s.at[i, d], n_r.at[i, r], y_peer(d), here, n_r.at[i, r],
                    )

        @each_head
        def _(h):
            QG[s, 0, :, head_cols(h)] = unit(ACC[:, head_cols(h)])
            for j in (2, 1):
                q_copy(s, h, j).start()

        if s == 1:
            keys_values()

    def q_copy(s, h, j):
        cols = head_cols(h)
        return remote(
            QG.at[s, 2 if j == 3 else 0, :, cols], QG.at[s, j, :, cols],
            q_s.at[s, j, h], q_r.at[s, j, h], class_peer(2 if j == 2 else 1),
        )

    def take_query(s, h, j):
        q_copy(s, h, j).wait_recv()

    def pass_query(s, h):
        take_query(s, h, 2)
        q_copy(s, h, 3).start()

    lane = lax.broadcasted_iota(jnp.int32, (256, 128), 1)

    def pack(l, m):
        return jnp.where(lane == 0, l, m)

    def unpack(st):
        both = jnp.concatenate([st] * 16, axis=0).T
        return both[:, 0:1], both[:, 1:2]

    def core_copy(s, h, k):
        at = (s, h, k)
        return remote(CS.at[at], CR.at[at], g_s.at[at], g_r.at[at], class_peer(1))

    def x_copies(s, h):
        at = (s, h)
        return (
            remote(PS.at[at], PR.at[at], p_s.at[at], p_r.at[at], class_peer(2)),
            remote(PST.at[at], PRT.at[at], t_s.at[at], t_r.at[at], class_peer(2)),
        )

    def attend(s, h, j):
        cols = head_cols(h)
        rows = [pl.ds(0 if i == 0 else 256, 1024) for i in (j, j + 1)]
        sc = [_dot_nt(QG[s, j + i, :, cols], KB[s, rows[i], cols]) for i in (0, 1)]
        m = [jnp.max(x, axis=-1, keepdims=True) if s == 0 else 0.0 for x in sc]
        p = [jnp.exp2((x - y) * C) if s == 0 else jnp.exp2(x * C) for x, y in zip(sc, m)]
        l = [jnp.sum(x, axis=-1, keepdims=True) for x in p]
        a = [_dot(p[i].astype(BF), VB[s, rows[i], cols]) for i in (0, 1)]
        k = j // 2
        CS[s, h, k, 0] = a[1]
        CS[s, h, k, 1] = pack(l[1], m[1])
        core_copy(s, h, k).start()
        LA[s, h, k, 0] = a[0]
        LA[s, h, k, 1] = pack(l[0], m[0])

    def add_up(s, parts):
        accs, ls, ms = zip(*parts)
        if s == 1:
            return sum(accs), sum(ls), 0.0
        top = functools.reduce(jnp.maximum, ms)
        ws = [jnp.exp2((m - top) * C) for m in ms]
        return sum(w * a for w, a in zip(ws, accs)), sum(w * l for w, l in zip(ws, ls)), top

    def near(s, h, k):
        core_copy(s, h, k).wait_recv()
        return [(ref[s, h, k, 0], ref[s, h, k, 1][:, 0:1], ref[s, h, k, 1][:, 1:2]) for ref in (LA, CR)]

    def combine(s, h):
        a, l, m = add_up(s, near(s, h, 1))
        PS[s, h] = a.astype(BF)
        PST[s, h] = pack(l, m).T[:8]
        for copy in x_copies(s, h):
            copy.start()

    def merge(s, h):
        parts = near(s, h, 0)
        for copy in x_copies(s, h):
            copy.wait_recv()
        a, l, _ = add_up(s, parts + [(PR[s, h].astype(F32),) + unpack(PRT[s, h])])
        AG[s, h, :, pl.ds(0, 128)] = (a / l).astype(BF)
        att_pass(s, h, OWN, ())

    def out_head(s, h):
        for slot, half in ((5, 0), (5, 1), (3, None), (7, None)):
            att_take(s, h, slot, half)
        OACC[s] += _dot(AG[s, h], WOG[h].reshape(1024, 640))

    def output_copy(s):
        return pltpu.make_async_copy(OACC.at[s], (out1, out2)[s], l_s.at[3 + s])

    def output(s):
        OACC[s] = jnp.zeros((256, 640), F32)
        each_head(functools.partial(out_head, s))
        output_copy(s).start()

    def settle(s):
        @each_head
        def _(h):
            for j in (1, 2, 3):
                q_copy(s, h, j).wait_send()
            for k in (0, 1):
                core_copy(s, h, k).wait_send()
            for copy in x_copies(s, h):
                copy.wait_send()
            for hop in OWN + SIDES + PARTNER:
                att_copy(s, h, hop).wait_send()

    def settle_last(s, h):
        for hop in OPPOSITE:
            att_copy(s, h, hop).wait_send()

    def wo_rows(yy):
        return pl.ds(pl.multiple_of((((y + yy) % 4) * 2 + c) * 16, 16), 16)

    def wo_first():
        for r in T_ORDER:
            m = mirror(r)
            cols = pl.ds(pl.multiple_of(t_index(r) * 640, 640), 640)
            send(
                ("o1", r), wo.at[:, wo_rows(0), cols], WOG.at[:, m, wo_rows(0)], o1_s.at[r], o1_r.at[m], t_peer(r),
                WOG.at[:, r, wo_rows(0)], o1_r.at[r],
            )

    def wo_first_wait():
        for r in T_ORDER:
            take("o1", r)

    def wo_piece(yy):
        return WOG.at[:, pl.ds(1, 7), wo_rows(yy)]

    def wo_third(yy):
        rows = pl.ds(pl.multiple_of((((y + yy) % 4) * 2 + (1 - c)) * 16, 16), 16)
        send(
            ("o3", yy), wo_piece(yy), wo_piece(yy), o3_s.at[yy], o3_r.at[yy], class_peer(1),
            WOG.at[:, pl.ds(1, 7), rows], o3_r.at[yy],
        )

    def wo_second():
        for d in Y_ORDER:
            r = 4 - d
            send(("o2", r), wo_piece(0), wo_piece(0), o2_s.at[d], o2_r.at[r], y_peer(d), wo_piece(r), o2_r.at[r])
        wo_third(0)

    def wo_relay():
        for r in Y_ORDER:
            take("o2", r)
            wo_third(r)

    def wo_last_wait():
        for yy in range(4):
            take("o3", yy)
        own_wo.wait()

    def heads(fn, *args):
        each_head(lambda h: fn(args[0], h, *args[1:]))

    lat_sides(0)
    lat_partner(0, 0)
    lat_partner(0, 1)
    lat_opposite(0)
    wo_first()
    project(0, 0, 5)
    start_latents(1)
    project(0, 5, 8)
    norms(0)
    own_k.wait()
    own_v.wait()
    for r in Y_ORDER:
        for i in range(2):
            take("c", i, r)
    lat_sides(1)
    lat_partner(1, 0)
    heads(take_query, 0, 1)
    heads(attend, 0, 0)
    lat_partner(1, 1)
    lat_opposite(1)
    heads(pass_query, 0)
    project(1, 0, 4)
    heads(take_query, 0, 3)
    heads(attend, 0, 2)
    wo_first_wait()
    wo_second()
    heads(combine, 0)
    project(1, 4, 8)
    norms(1)
    for r in Y_ORDER:
        for i in range(2):
            take("n", i, r)
    heads(merge, 0)
    for h in range(3):
        take_query(1, h, 1)
        attend(1, h, 0)
        if h:
            pass_query(1, h - 1)
    pass_query(1, 2)
    for h in range(3):
        take_query(1, h, 3)
        attend(1, h, 2)
        if h:
            combine(1, h - 1)
    combine(1, 2)
    heads(att_first, 0)
    heads(merge, 1)
    heads(att_second, 0)
    heads(att_first, 1)
    wo_relay()
    heads(att_second, 1)
    settle(0)
    heads(settle_last, 0)
    for cp in sends:
        cp.wait_send()
    wo_last_wait()
    output(0)
    settle(1)
    output(1)
    heads(settle_last, 1)
    output_copy(0).wait()
    output_copy(1).wait()


def _shards(latent_first, latent_second, stale_keys, stale_values, w_query, w_key, w_value, w_output):
    dma = pltpu.SemaphoreType.DMA
    vm = pltpu.VMEM
    scratch = [
        vm((2, 8, 256, 640), BF),
        vm((8, 640, 1152), BF),
        vm((256, 1152), F32),
        vm((256, 128), F32),
        vm((2, 4, 256, 384), BF),
        vm((2, 1280, 384), BF),
        vm((2, 1280, 384), BF),
        vm((2, 3, 2, 2, 256, 128), F32),
        vm((2, 3, 2, 2, 256, 128), F32),
        vm((2, 3, 2, 2, 256, 128), F32),
        vm((2, 3, 256, 128), BF),
        vm((2, 3, 256, 128), BF),
        vm((2, 3, 8, 256), F32),
        vm((2, 3, 8, 256), F32),
        vm((2, 3, 256, 1024), BF),
        vm((3, 8, 128, 640), BF),
        vm((2, 256, 640), F32),
        dma((2, 16)), dma((2, 16)),
        dma((8, 3)),
        dma((2, 4)), dma((2, 4)),
        dma((2, 4)), dma((2, 4)),
        dma((2, 4, 3)), dma((2, 4, 3)),
        dma((2, 3)), dma((2, 3)),
        dma((2, 3)), dma((2, 3)),
        dma((2, 3, 2)), dma((2, 3, 2)),
        dma((2, 3, 10)), dma((2, 3, 10)),
        dma((8,)), dma((8,)),
        dma((4,)), dma((4,)),
        dma((4,)), dma((4,)),
        dma((5,)),
    ]
    out = jax.ShapeDtypeStruct((256, 640), F32)
    sums = pl.pallas_call(
        _kernel,
        out_shape=(out, out),
        in_specs=[pl.BlockSpec(memory_space=pl.ANY)] * 8,
        out_specs=(pl.BlockSpec(memory_space=pl.ANY),) * 2,
        scratch_shapes=scratch,
        compiler_params=pltpu.CompilerParams(
            collective_id=0, has_side_effects=True, vmem_limit_bytes=60 * 2**20
        ),
        cost_estimate=pl.CostEstimate(flops=11_300_000_000, bytes_accessed=20_000_000, transcendentals=6_300_000),
        name="patch_attention",
    )(
        latent_first, latent_second, stale_keys, stale_values,
        w_query, w_key, w_value, w_output.reshape(3, 128, 5120),
    )
    return tuple((x.astype(F32) + part).astype(BF) for x, part in zip((latent_first, latent_second), sums))


def solution(mesh):
    in_specs = (
        P("patch", "tensor"),
        P("patch", "tensor"),
        P("patch", "tensor"),
        P("patch", "tensor"),
        P(None, "tensor"),
        P(None, "tensor"),
        P(None, "tensor"),
        P("tensor", None),
    )
    out_specs = (P("patch", "tensor"), P("patch", "tensor"))
    return jax.shard_map(_shards, mesh=mesh, in_specs=in_specs, out_specs=out_specs, check_vma=False)
```
